256 devices in a mesh: expert: 128 (over x, z_hi, y, core), hid: 2 (over z_lo).
Axes of the slice: x: 4, y: 4, z: 8 (z_hi: 4, z_lo: 2; z = z_hi * 2 + z_lo), core: 2. Of those that a mesh axis runs over, the one named last changes fastest.
Arguments:
- tokens: bfloat16 [256, 196, 768], P(('expert', 'hid')), may hold values from -6 to 6
- grad_out: bfloat16 [256, 196, 768], P(('expert', 'hid')), may hold values from -6 to 6
- slot_param: bfloat16 [768, 256], replicated, may hold values from -0.6 to 0.6
- weight_in: bfloat16 [128, 768, 3072], P('expert', None, 'hid'), may hold values from -0.21875 to 0.21875
- weight_out: bfloat16 [128, 3072, 768], P('expert', 'hid'), may hold values from -0.109375 to 0.109375
Outputs:
- grad_tokens: float32 [256, 196, 768], P(('expert', 'hid'))
- grad_weight_in: bfloat16 [128, 768, 3072], P('expert', None, 'hid')
- grad_weight_out: bfloat16 [128, 3072, 768], P('expert', 'hid')
- grad_slot_param: float32 [768, 256], replicated
The draws below stay inside these ranges and needn't reach their ends.
All inputs are finite; a program needn't handle non-finite values.
Results may differ from the reference program's by a relative error of at most 0.015.
Values may be sent and summed in bfloat16 or wider, within the bound.
A program may use at most 64 MiB of HBM per device.

```python
import jax
import jax.numpy as jnp
from jax import lax

D = 768
H = 3072
M = 196
PER_EXPERT = 2
EXPERTS = 128
SLOTS = 256
IMAGES = 256


def draw_tokens(key, part):
    key = jax.random.fold_in(key, 11)
    first = jax.random.fold_in(key, 0)
    base = jax.random.normal(first, (IMAGES, M, D), jnp.float32)
    return jnp.clip(base, -6.0, 6.0).astype(jnp.bfloat16)


def draw_slot_param(key, part):
    key = jax.random.fold_in(key, 23)
    first = jax.random.fold_in(key, 0)
    base = jax.random.normal(first, (D, SLOTS), jnp.float32) * D ** (-0.5)
    return jnp.clip(base, -0.59375, 0.59375).astype(jnp.bfloat16)


def shard_levels(key, extent, cuts, low, top_value):
    def one(axis_at, blocks):
        heights = jax.random.uniform(jax.random.fold_in(jax.random.fold_in(key, 6), axis_at), (blocks,), jnp.float32, low / len(cuts), top_value / len(cuts))
        return jnp.repeat(jnp.exp(heights), extent[axis_at] // blocks).reshape((-1,) + (1,) * (len(extent) - axis_at - 1))

    factor_of = one(*cuts[0])
    for cut in cuts[1:]:
        factor_of = factor_of * one(*cut)
    return factor_of


def centred(own_key, dims, deviation, most, cuts=(), kind=jnp.bfloat16):
    result = deviation * jax.random.normal(own_key, dims, jnp.float32)
    if cuts:
        result = result * shard_levels(own_key, dims, cuts, -0.22, 0.18)
    return jnp.clip(result, -most, most).astype(kind)


def setup_inputs(seed: int = 0) -> dict:
    arg_keys = jax.random.split(jax.random.key(seed), 6)
    tokens = draw_tokens(jax.random.fold_in(arg_keys[5], 71), 0)
    grad_out = centred(arg_keys[1], (IMAGES, M, D), 1.0, 6.0, ((0, 256),))
    slot_param = draw_slot_param(jax.random.fold_in(arg_keys[5], 71), 0)
    weight_in = centred(arg_keys[3], (EXPERTS, D, H), D ** -0.5, 0.21875, ((0, 128), (2, 2)))
    weight_out = centred(arg_keys[4], (EXPERTS, H, D), H ** -0.5, 0.109375, ((0, 128), (1, 2)))
    return dict(tokens=tokens, grad_out=grad_out, slot_param=slot_param, weight_in=weight_in, weight_out=weight_out)


def gelu_tanh(value):
    return jax.nn.gelu(value, approximate=True)

def expert_pass(operands):
    slot_rows, grad_rows, weight_first, weight_second = operands
    pre_act = jnp.dot(slot_rows, weight_first, preferred_element_type=jnp.float32)
    hidden_act = gelu_tanh(pre_act).astype(jnp.bfloat16)
    slot_result = jnp.dot(hidden_act, weight_second, preferred_element_type=jnp.float32).astype(jnp.bfloat16)
    grad_second = jnp.dot(hidden_act.T, grad_rows, preferred_element_type=jnp.float32).astype(jnp.bfloat16)
    grad_hidden = jnp.dot(grad_rows, weight_second.T, preferred_element_type=jnp.float32)
    grad_pre = jax.vjp(gelu_tanh, pre_act)[1](grad_hidden)[0].astype(jnp.bfloat16)
    grad_first = jnp.dot(slot_rows.T, grad_pre, preferred_element_type=jnp.float32).astype(jnp.bfloat16)
    grad_slot_rows = jnp.dot(grad_pre, weight_first.T, preferred_element_type=jnp.float32).astype(jnp.bfloat16)
    return (slot_result, grad_first, grad_second, grad_slot_rows)

def to_experts(slot_data):
    shaped = slot_data.reshape(IMAGES, EXPERTS, PER_EXPERT, D)
    return jnp.transpose(shaped, (1, 0, 2, 3)).reshape(EXPERTS, IMAGES * PER_EXPERT, D)

def from_experts(expert_data):
    shaped = expert_data.reshape(EXPERTS, IMAGES, PER_EXPERT, D)
    return jnp.transpose(shaped, (1, 0, 2, 3)).reshape(IMAGES, SLOTS, D)

def reference(tokens, grad_out, slot_param, weight_in, weight_out):
    f32 = jnp.float32
    bf16 = jnp.bfloat16
    logits = jnp.einsum('bmd,dn->bmn', tokens.astype(f32), slot_param.astype(f32))
    dispatch = jax.nn.softmax(logits, axis=1)
    combine = jax.nn.softmax(logits, axis=2)
    dispatch_b = dispatch.astype(bf16)
    combine_b = combine.astype(bf16)
    slot_in = jnp.einsum('bmn,bmd->bnd', dispatch_b.astype(f32), tokens.astype(f32)).astype(bf16)
    grad_slot_out = jnp.einsum('bmn,bmd->bnd', combine_b.astype(f32), grad_out.astype(f32)).astype(bf16)
    slot_out, grad_weight_in, grad_weight_out, grad_slot_in = lax.map(expert_pass, (to_experts(slot_in), to_experts(grad_slot_out), weight_in, weight_out))
    slot_out = from_experts(slot_out)
    grad_slot_in = from_experts(grad_slot_in)
    grad_combine = jnp.einsum('bmd,bnd->bmn', grad_out.astype(f32), slot_out.astype(f32))
    part_combine = (combine * (grad_combine - lax.optimization_barrier(jnp.sum(grad_combine * combine, axis=2, keepdims=True)))).astype(bf16)
    grad_dispatch = jnp.einsum('bmd,bnd->bmn', tokens.astype(f32), grad_slot_in.astype(f32))
    part_dispatch = (dispatch * (grad_dispatch - lax.optimization_barrier(jnp.sum(grad_dispatch * dispatch, axis=1, keepdims=True)))).astype(bf16)
    slot_wide = slot_param.astype(f32)
    grad_tokens = jnp.einsum('bmn,bnd->bmd', dispatch_b.astype(f32), grad_slot_in.astype(f32))
    grad_tokens = grad_tokens + jnp.einsum('bmn,dn->bmd', part_combine.astype(f32), slot_wide)
    grad_tokens = grad_tokens + jnp.einsum('bmn,dn->bmd', part_dispatch.astype(f32), slot_wide)
    grad_slot_param = jnp.einsum('bmd,bmn->dn', tokens.astype(f32), part_combine.astype(f32))
    grad_slot_param = grad_slot_param + jnp.einsum('bmd,bmn->dn', tokens.astype(f32), part_dispatch.astype(f32))
    return (grad_tokens, grad_weight_in, grad_weight_out, grad_slot_param)
```

```python
import math

import jax
import jax.numpy as jnp
from jax import lax
from jax.experimental import pallas as pl
from jax.experimental.pallas import tpu as pltpu
from jax.sharding import PartitionSpec as P

F32 = jnp.float32
BF16 = jnp.bfloat16
MESH = pl.DeviceIdType.MESH

TOKENS = 196
PAD = 208
WIDTH = 768
HALF_HIDDEN = 1536
SLOTS = 256
ROWS = 512
NEAR = 256
BLOCK = 32
TILE = 256
ROOT = math.sqrt(2.0 / math.pi)


def dot(left, right, left_dim=1, right_dim=0):
    return lax.dot_general(
        left, right, (((left_dim,), (right_dim,)), ((), ())), preferred_element_type=F32
    )


def one_hot(rows, columns, source):
    row = lax.broadcasted_iota(jnp.int32, (rows, columns), 0)
    column = lax.broadcasted_iota(jnp.int32, (rows, columns), 1)
    return jnp.where(source(row) == column, 1.0, 0.0).astype(BF16)


def swap_slots(index):
    return (index & 0xC3) | ((index & 0x30) >> 2) | ((index & 0x0C) << 2)


def to_line(index):
    return (((index >> 1) & 15) << 4) | ((index >> 5) << 1) | (index & 1)


def to_plane(index):
    return (((index >> 1) & 7) << 5) | ((index >> 4) << 1) | (index & 1)


def kernel(
    tok_ref,
    go_ref,
    sp_ref,
    win_hbm,
    wout_hbm,
    gt_ref,
    gwi_hbm,
    gwo_hbm,
    gsp_ref,
    tok,
    go,
    tok_t,
    spp,
    disp,
    comb,
    disp_b,
    win,
    wout,
    plane_out,
    plane_in,
    line_out,
    line_in,
    rows,
    twin_out,
    twin_in,
    own,
    act,
    slope,
    gpre,
    gwi,
    gwo,
    acc_t,
    grad,
    grad_core,
    ar_out,
    ar_in,
    z_out,
    z_in,
    done,
    w_sem,
    o_sem,
    p_send,
    p_recv,
    l_send,
    l_recv,
    f_send,
    f_recv,
    c_send,
    c_recv,
    a_send,
    a_recv,
    g_send,
    g_recv,
    z_send,
    z_recv,
):
    expert = lax.axis_index("expert")
    zl = lax.axis_index("hid")
    x = expert >> 5
    zh = (expert >> 3) & 3
    y = (expert >> 1) & 3
    c = expert & 1
    z = zh * 2 + zl
    mine = x * 4 + y
    side = 2 * zl - 1

    def device(px, py, pz, pc):
        return {
            "expert": (((px * 4 + (pz >> 1)) * 4 + py) * 2) + pc,
            "hid": pz & 1,
        }

    twin = device(x, y, z ^ 1, c)
    sibling = device(x, y, z, c ^ 1)

    def plane_peer(k):
        return (x + (k >> 2)) & 3, (y + (k & 3)) & 3

    w_copies = [
        pltpu.make_async_copy(win_hbm.at[0], win, w_sem.at[0]),
        pltpu.make_async_copy(wout_hbm.at[0], wout, w_sem.at[1]),
    ]
    for copy in w_copies:
        copy.start()

    barrier = pltpu.get_barrier_semaphore()

    @pl.loop(1, 16)
    def _(k):
        px, py = plane_peer(k)
        pl.semaphore_signal(barrier, inc=1, device_id=device(px, py, z, c), device_id_type=MESH)
        pl.semaphore_signal(
            barrier,
            inc=1,
            device_id=device(x, y, (z + (k >> 1)) & 7, c ^ (k & 1)),
            device_id_type=MESH,
        )

    def block16(index):
        return pl.ds(pl.multiple_of(index * 16, 16), 16)

    def block32(index):
        return pl.ds(pl.multiple_of(index * BLOCK, BLOCK), BLOCK)

    def plane_copy(a, k):
        px, py = plane_peer(k)
        return pltpu.make_async_remote_copy(
            src_ref=plane_out.at[a, block16(px * 4 + py)],
            dst_ref=plane_in.at[a, block16(mine)],
            send_sem=p_send.at[a, k],
            recv_sem=p_recv.at[a, k],
            device_id=device(px, py, z, c),
            device_id_type=MESH,
        )

    def plane_start(a):
        @pl.loop(1, 16)
        def _(k):
            plane_copy(a, k).start()

        plane_in[a, block16(mine)] = plane_out[a, block16(mine)]

    def plane_finish(a):
        @pl.loop(1, 16)
        def _(k):
            plane_copy(a, k).wait_recv()

    def line_copy(a, j):
        q = (zh + (j >> 1)) & 3
        pc = c ^ (j & 1)
        k = (z - 2 * q + 11) & 7
        low = k >> 2
        far = jnp.where(low == 1, k - 4, 3 - k)
        return pltpu.make_async_remote_copy(
            src_ref=line_out.at[a, block32(q * 2 + pc)],
            dst_ref=rows.at[a, block32(k * 2 + c)],
            send_sem=l_send.at[a, j],
            recv_sem=l_recv.at[a, far * 2 + (j & 1)],
            device_id=device(x, y, 2 * q + low, pc),
            device_id_type=MESH,
        )

    def near_row(t, pc):
        return (3 + zl + side * t) * 2 + pc

    def line_start(a):
        @pl.loop(1, 8)
        def _(j):
            line_copy(a, j).start()

        rows[a, block32((3 + zl) * 2 + c)] = line_out[a, block32(zh * 2 + c)]

    def arrive(a, j):
        place = block32(near_row(j >> 1, c ^ (j & 1)))
        return pltpu.make_async_remote_copy(
            src_ref=rows.at[a, place],
            dst_ref=rows.at[a, place],
            send_sem=f_send.at[a, j],
            recv_sem=l_recv.at[a, j],
            device_id=twin,
            device_id_type=MESH,
        )

    def forward(a, j):
        place = block32(near_row(j >> 1, c ^ (j & 1)))
        return pltpu.make_async_remote_copy(
            src_ref=rows.at[a, place],
            dst_ref=rows.at[a, place],
            send_sem=f_send.at[a, j],
            recv_sem=f_recv.at[a, j],
            device_id=twin,
            device_id_type=MESH,
        )

    def pass_on(a):
        forward(a, 0).start()

        @pl.loop(1, 8)
        def _(j):
            arrive(a, j).wait_recv()
            forward(a, j).start()

    def far_finish(a):
        @pl.loop(0, 8)
        def _(j):
            forward(a, j).wait_recv()

    def twin_copy(a, t):
        place = pl.ds(pl.multiple_of(t * 64, 64), 64)
        return pltpu.make_async_remote_copy(
            src_ref=twin_out.at[a, place],
            dst_ref=twin_in.at[a, place],
            send_sem=c_send.at[a, t],
            recv_sem=c_recv.at[a, t],
            device_id=twin,
            device_id_type=MESH,
        )

    def back_copy(a, j):
        t = j >> 1
        pc = c ^ (j & 1)
        pz = (z + side * t + 8) & 7
        shift = (zh - (pz >> 1) + 4) & 3
        return pltpu.make_async_remote_copy(
            src_ref=line_out.at[2 + a, block32(near_row(t, pc) - 8 * zl)],
            dst_ref=line_in.at[a, block32(zh * 2 + c)],
            send_sem=l_send.at[2 + a, j],
            recv_sem=l_recv.at[2 + a, shift * 2 + (j & 1)],
            device_id=device(x, y, pz, pc),
            device_id_type=MESH,
        )

    near_rows = pl.ds(pl.multiple_of(zl * NEAR, NEAR), NEAR)
    far_rows = pl.ds(pl.multiple_of((1 - zl) * NEAR, NEAR), NEAR)

    def back_finish(a):
        @pl.loop(1, 8)
        def _(j):
            pltpu.make_async_remote_copy(
                src_ref=line_in.at[a, block32(0)],
                dst_ref=line_in.at[a, block32(0)],
                send_sem=l_send.at[2 + a, j],
                recv_sem=l_recv.at[2 + a, j],
                device_id=twin,
                device_id_type=MESH,
            ).wait_recv()

    tok[...] = jnp.zeros_like(tok)
    tok[0:TOKENS, :] = tok_ref[0]
    go[...] = jnp.zeros_like(go)
    go[0:TOKENS, :] = go_ref[0]
    swap = one_hot(SLOTS, SLOTS, swap_slots)
    spp[...] = dot(sp_ref[...], swap).astype(BF16)
    logits = dot(tok[...], spp[...])
    valid = lax.broadcasted_iota(jnp.int32, (PAD, SLOTS), 0) < TOKENS
    masked = jnp.where(valid, logits, -1e30)
    raised = jnp.exp(masked - jnp.max(masked, axis=0, keepdims=True))
    dispatch = raised / jnp.sum(raised, axis=0, keepdims=True)
    disp[...] = dispatch
    disp_b[...] = dispatch.astype(BF16)
    plane_out[0] = dot(disp_b[...], tok[...], 0, 0).astype(BF16)
    pl.semaphore_wait(barrier, 30)
    plane_start(0)
    raised = jnp.exp(logits - jnp.max(logits, axis=1, keepdims=True))
    combine = raised / jnp.sum(raised, axis=1, keepdims=True)
    comb[...] = combine
    plane_out[1] = dot(combine.astype(BF16), go[...], 0, 0).astype(BF16)
    plane_start(1)
    tok_t[...] = tok[...].T

    line = one_hot(SLOTS, SLOTS, to_line)
    for a in range(2):
        plane_finish(a)
        line_out[a] = dot(line, plane_in[a]).astype(BF16)
        line_start(a)
    pass_on(0)
    for copy in w_copies:
        copy.wait()
    far_finish(0)

    @pl.loop(0, HALF_HIDDEN // TILE)
    def _(j):
        tile = pl.ds(pl.multiple_of(j * TILE, TILE), TILE)
        pre = dot(rows[0], win[:, tile])
        square = pre * pre
        tanh = jnp.tanh(ROOT * pre * (1.0 + 0.044715 * square))
        half = 0.5 * (1.0 + tanh)
        act[:, tile] = (pre * half).astype(BF16)
        slope[:, tile] = half + (0.5 * ROOT) * pre * (1.0 - tanh * tanh) * (
            1.0 + (3 * 0.044715) * square
        )

    def send_back(a, wide, weight, weight_dim):
        def piece(place, j):
            tile = pl.ds(pl.multiple_of(j * TILE, TILE), TILE)
            if weight_dim == 0:
                return tile, dot(wide[place], weight[:, tile])
            return tile, dot(wide[place], weight[tile, :], 1, 1)

        @pl.loop(0, WIDTH // TILE)
        def _(j):
            tile, value = piece(far_rows, j)
            twin_out[a, :, tile] = value.astype(BF16)

        @pl.loop(0, 4)
        def _(t):
            twin_copy(a, t).start()

        @pl.loop(0, WIDTH // TILE)
        def _(j):
            tile, value = piece(near_rows, j)
            own[:, tile] = value

    def sum_back(a):
        @pl.loop(0, 4)
        def _(t):
            twin_copy(a, t).wait_recv()

        line_out[2 + a] = (own[...] + twin_in[a].astype(F32)).astype(BF16)

        @pl.loop(1, 8)
        def _(j):
            back_copy(a, j).start()

        line_in[a, block32(zh * 2 + c)] = line_out[2 + a, block32(near_row(0, c) - 8 * zl)]

    send_back(0, act, wout, 0)
    pass_on(1)
    sum_back(0)
    far_finish(1)

    @pl.loop(0, HALF_HIDDEN // TILE)
    def _(j):
        tile = pl.ds(pl.multiple_of(j * TILE, TILE), TILE)
        gpre[:, tile] = (dot(rows[1], wout[tile, :], 1, 1) * slope[:, tile]).astype(BF16)

    send_back(1, gpre, win, 1)
    plane = one_hot(SLOTS, SLOTS, to_plane)
    back_finish(0)
    plane_out[2] = dot(plane, line_in[0]).astype(BF16)
    plane_start(2)
    sum_back(1)

    def out_copies(j):
        tile = pl.ds(pl.multiple_of(j * TILE, TILE), TILE)
        return pltpu.make_async_copy(gwo.at[tile], gwo_hbm.at[0, tile], o_sem.at[0, j])

    def in_copies(j):
        tile = pl.ds(pl.multiple_of(j * TILE, TILE), TILE)
        return pltpu.make_async_copy(gwi.at[tile], gwi_hbm.at[0, tile], o_sem.at[1, j])

    @pl.loop(0, HALF_HIDDEN // TILE)
    def _(j):
        tile = pl.ds(pl.multiple_of(j * TILE, TILE), TILE)
        gwo[tile, :] = dot(act[:, tile], rows[1], 0, 0).astype(BF16)
        out_copies(j).start()

    @pl.loop(0, WIDTH // TILE)
    def _(j):
        tile = pl.ds(pl.multiple_of(j * TILE, TILE), TILE)
        gwi[tile, :] = dot(rows[0, :, tile], gpre[...], 0, 0).astype(BF16)
        in_copies(j).start()

    back_finish(1)
    plane_out[3] = dot(plane, line_in[1]).astype(BF16)
    plane_start(3)
    plane_finish(2)
    gc = dot(go[...], plane_in[2], 1, 1)
    weight = comb[...]
    part = dot(
        (weight * (gc - jnp.sum(gc * weight, axis=1, keepdims=True))).astype(BF16), swap
    ).astype(BF16)
    acc_t[...] = dot(part, sp_ref[...], 1, 1)
    grad_half = dot(tok_t[...], part)
    grad[0] = grad_half[:, 0:128]
    grad[1] = grad_half[:, 128:256]
    plane_finish(3)
    gd = dot(tok[...], plane_in[3], 1, 1)
    weight = disp[...]
    part = dot(
        (weight * (gd - jnp.sum(gd * weight, axis=0, keepdims=True))).astype(BF16), swap
    ).astype(BF16)
    grad_half = dot(tok_t[...], part)
    grad[0] += grad_half[:, 0:128]
    grad[1] += grad_half[:, 128:256]

    core_copy = pltpu.make_async_remote_copy(
        src_ref=grad.at[c ^ 1],
        dst_ref=grad_core,
        send_sem=g_send.at[0],
        recv_sem=g_recv.at[0],
        device_id=sibling,
        device_id_type=MESH,
    )
    core_copy.start()
    total = acc_t[...] + dot(part, sp_ref[...], 1, 1) + dot(disp_b[...], plane_in[3])
    gt_ref[0] = total[0:TOKENS]
    core_copy.wait_recv()
    ar_out[...] = (grad[c] + grad_core[...]).astype(BF16)

    def block48(index):
        return pl.ds(pl.multiple_of(index * 48, 48), 48)

    def reduce_copy(k):
        px, py = plane_peer(k)
        return pltpu.make_async_remote_copy(
            src_ref=ar_out.at[block48(px * 4 + py)],
            dst_ref=ar_in.at[block48(mine)],
            send_sem=a_send.at[0, k],
            recv_sem=a_recv.at[0, k],
            device_id=device(px, py, z, c),
            device_id_type=MESH,
        )

    @pl.loop(1, 16)
    def _(k):
        reduce_copy(k).start()

    ar_in[block48(mine)] = ar_out[block48(mine)]

    @pl.loop(1, 16)
    def _(k):
        reduce_copy(k).wait_recv()

    plane_sum = ar_in[0:48].astype(F32)
    for k in range(1, 16):
        plane_sum += ar_in[48 * k : 48 * k + 48].astype(F32)
    z_out[...] = plane_sum.astype(BF16)

    def z_copy(k):
        return pltpu.make_async_remote_copy(
            src_ref=z_out,
            dst_ref=z_in.at[z],
            send_sem=z_send.at[k],
            recv_sem=z_recv.at[k],
            device_id=device(x, y, (z + k) & 7, c),
            device_id_type=MESH,
        )

    @pl.loop(1, 8)
    def _(k):
        z_copy(k).start()

    z_in[z] = z_out[...]

    @pl.loop(1, 8)
    def _(k):
        z_copy(k).wait_recv()

    line_sum = z_in[0].astype(F32)
    for k in range(1, 8):
        line_sum += z_in[k].astype(F32)
    done[c, block48(mine)] = line_sum

    def gather_copy(k):
        px, py = plane_peer(k)
        return pltpu.make_async_remote_copy(
            src_ref=done.at[c, block48(mine)],
            dst_ref=done.at[c, block48(mine)],
            send_sem=a_send.at[1, k],
            recv_sem=a_recv.at[1, k],
            device_id=device(px, py, z, c),
            device_id_type=MESH,
        )

    @pl.loop(1, 16)
    def _(k):
        gather_copy(k).start()

    @pl.loop(1, 16)
    def _(k):
        gather_copy(k).wait_recv()

    last_copy = pltpu.make_async_remote_copy(
        src_ref=done.at[c],
        dst_ref=done.at[c],
        send_sem=g_send.at[1],
        recv_sem=g_recv.at[1],
        device_id=sibling,
        device_id_type=MESH,
    )
    last_copy.start()

    @pl.loop(1, 16)
    def _(k):
        for a in range(4):
            plane_copy(a, k).wait_send()
        reduce_copy(k).wait_send()
        gather_copy(k).wait_send()

    @pl.loop(1, 8)
    def _(k):
        z_copy(k).wait_send()
        for a in range(2):
            line_copy(a, k).wait_send()
            back_copy(a, k).wait_send()

    @pl.loop(0, 8)
    def _(k):
        for a in range(2):
            forward(a, k).wait_send()

    @pl.loop(0, 4)
    def _(t):
        for a in range(2):
            twin_copy(a, t).wait_send()

    core_copy.wait_send()

    @pl.loop(0, HALF_HIDDEN // TILE)
    def _(j):
        out_copies(j).wait()

    @pl.loop(0, WIDTH // TILE)
    def _(j):
        in_copies(j).wait()

    last_copy.wait()
    gsp_ref[:, 0:128] = done[0]
    gsp_ref[:, 128:256] = done[1]


def body(tokens, grad_out, slot_param, weight_in, weight_out):
    vmem = pl.BlockSpec(memory_space=pltpu.VMEM)
    hbm = pl.BlockSpec(memory_space=pl.ANY)
    dma = pltpu.SemaphoreType.DMA
    buffers = [
        ((PAD, WIDTH), BF16),
        ((PAD, WIDTH), BF16),
        ((WIDTH, PAD), BF16),
        ((WIDTH, SLOTS), BF16),
        ((PAD, SLOTS), F32),
        ((PAD, SLOTS), F32),
        ((PAD, SLOTS), BF16),
        ((WIDTH, HALF_HIDDEN), BF16),
        ((HALF_HIDDEN, WIDTH), BF16),
        ((4, SLOTS, WIDTH), BF16),
        ((4, SLOTS, WIDTH), BF16),
        ((4, SLOTS, WIDTH), BF16),
        ((2, SLOTS, WIDTH), BF16),
        ((2, ROWS, WIDTH), BF16),
        ((2, NEAR, WIDTH), BF16),
        ((2, NEAR, WIDTH), BF16),
        ((NEAR, WIDTH), F32),
        ((ROWS, HALF_HIDDEN), BF16),
        ((ROWS, HALF_HIDDEN), F32),
        ((ROWS, HALF_HIDDEN), BF16),
        ((WIDTH, HALF_HIDDEN), BF16),
        ((HALF_HIDDEN, WIDTH), BF16),
        ((PAD, WIDTH), F32),
        ((2, WIDTH, 128), F32),
        ((WIDTH, 128), F32),
        ((WIDTH, 128), BF16),
        ((WIDTH, 128), BF16),
        ((48, 128), BF16),
        ((8, 48, 128), BF16),
        ((2, WIDTH, 128), F32),
    ]
    return pl.pallas_call(
        kernel,
        out_shape=(
            jax.ShapeDtypeStruct(tokens.shape, F32),
            jax.ShapeDtypeStruct(weight_in.shape, BF16),
            jax.ShapeDtypeStruct(weight_out.shape, BF16),
            jax.ShapeDtypeStruct(slot_param.shape, F32),
        ),
        in_specs=[vmem, vmem, vmem, hbm, hbm],
        out_specs=(vmem, hbm, hbm, vmem),
        scratch_shapes=[pltpu.VMEM(shape, kind) for shape, kind in buffers]
        + [
            dma((2,)),
            dma((2, 8)),
            dma((4, 16)),
            dma((4, 16)),
            dma((4, 8)),
            dma((4, 8)),
            dma((2, 8)),
            dma((2, 8)),
            dma((2, 4)),
            dma((2, 4)),
            dma((2, 16)),
            dma((2, 16)),
            dma((2,)),
            dma((2,)),
            dma((8,)),
            dma((8,)),
        ],
        compiler_params=pltpu.CompilerParams(
            collective_id=0, has_side_effects=True, vmem_limit_bytes=56 * 1024 * 1024
        ),
    )(tokens, grad_out, slot_param, weight_in, weight_out)


def solution(mesh):
    return jax.shard_map(
        body,
        mesh=mesh,
        in_specs=(
            P(("expert", "hid"), None, None),
            P(("expert", "hid"), None, None),
            P(),
            P("expert", None, "hid"),
            P("expert", "hid", None),
        ),
        out_specs=(
            P(("expert", "hid"), None, None),
            P("expert", None, "hid"),
            P("expert", "hid", None),
            P(),
        ),
        check_vma=False,
    )
```

```python
import math

import jax
import jax.numpy as jnp
from jax import lax
from jax.experimental import pallas as pl
from jax.experimental.pallas import tpu as pltpu
from jax.sharding import PartitionSpec as P

F32 = jnp.float32
BF16 = jnp.bfloat16
MESH = pl.DeviceIdType.MESH

TOKENS = 196
PAD = 208
WIDTH = 768
HALF_HIDDEN = 1536
SLOTS = 256
ROWS = 512
NEAR = 256
BLOCK = 32
HALF = 384
TILE = 256
ROOT = math.sqrt(2.0 / math.pi)


def dot(left, right, left_dim=1, right_dim=0):
    return lax.dot_general(
        left, right, (((left_dim,), (right_dim,)), ((), ())), preferred_element_type=F32
    )


def one_hot(rows, columns, source):
    row = lax.broadcasted_iota(jnp.int32, (rows, columns), 0)
    column = lax.broadcasted_iota(jnp.int32, (rows, columns), 1)
    return jnp.where(source(row) == column, 1.0, 0.0).astype(BF16)


def swap_slots(index):
    return (index & 0xC3) | ((index & 0x30) >> 2) | ((index & 0x0C) << 2)


def to_line(index):
    return (((index >> 1) & 15) << 4) | ((index >> 5) << 1) | (index & 1)


def to_plane(index):
    return (((index >> 1) & 7) << 5) | ((index >> 4) << 1) | (index & 1)


def kernel(
    tok_hbm,
    go_hbm,
    sp_hbm,
    win_hbm,
    wout_hbm,
    gt_hbm,
    gwi_hbm,
    gwo_hbm,
    gsp_hbm,
    tok_ref,
    go_ref,
    sp_ref,
    line,
    plane,
    swap,
    part_s,
    gt,
    gsp,
    tok,
    go,
    tok_t,
    spp,
    disp,
    comb,
    disp_b,
    win,
    wout,
    plane_out,
    plane_in,
    line_out,
    line_in,
    rows,
    twin_out,
    twin_in,
    own,
    act,
    slope,
    gpre,
    gwi,
    gwo,
    acc_t,
    grad,
    core_out,
    core_in,
    ar_out,
    ar_in,
    z_out,
    z_in,
    done,
    w_sem,
    o_sem,
    p_send,
    p_recv,
    l_send,
    l_recv,
    f_send,
    f_recv,
    c_send,
    c_recv,
    a_send,
    a_recv,
    g_send,
    g_recv,
    z_send,
    z_recv,
):
    expert = lax.axis_index("expert")
    zl = lax.axis_index("hid")
    x = expert >> 5
    zh = (expert >> 3) & 3
    y = (expert >> 1) & 3
    c = expert & 1
    z = zh * 2 + zl
    mine = x * 4 + y
    side = 2 * zl - 1

    def device(px, py, pz, pc):
        return {
            "expert": (((px * 4 + (pz >> 1)) * 4 + py) * 2) + pc,
            "hid": pz & 1,
        }

    twin = device(x, y, z ^ 1, c)
    sibling = device(x, y, z, c ^ 1)

    def plane_peer(k):
        return (x + (k >> 2)) & 3, (y + (k & 3)) & 3

    i_copies = [
        pltpu.make_async_copy(sp_hbm, sp_ref, w_sem.at[2]),
        pltpu.make_async_copy(tok_hbm, tok_ref, w_sem.at[3]),
        pltpu.make_async_copy(go_hbm, go_ref, w_sem.at[4]),
    ]
    w_copies = [
        pltpu.make_async_copy(win_hbm.at[0], win, w_sem.at[0]),
        pltpu.make_async_copy(wout_hbm.at[0], wout, w_sem.at[1]),
    ]
    for copy in i_copies + w_copies:
        copy.start()

    barrier = pltpu.get_barrier_semaphore()

    @pl.loop(1, 16)
    def _(k):
        px, py = plane_peer(k)
        pl.semaphore_signal(barrier, inc=1, device_id=device(px, py, z, c), device_id_type=MESH)
        pl.semaphore_signal(
            barrier,
            inc=1,
            device_id=device(x, y, (z + (k >> 1)) & 7, c ^ (k & 1)),
            device_id_type=MESH,
        )

    def block16(index):
        return pl.ds(pl.multiple_of(index * 16, 16), 16)

    def block32(index):
        return pl.ds(pl.multiple_of(index * BLOCK, BLOCK), BLOCK)

    def plane_copy(a, k):
        px, py = plane_peer(k)
        return pltpu.make_async_remote_copy(
            src_ref=plane_out.at[a, block16(px * 4 + py)],
            dst_ref=plane_in.at[a, block16(mine)],
            send_sem=p_send.at[a, k],
            recv_sem=p_recv.at[a, k],
            device_id=device(px, py, z, c),
            device_id_type=MESH,
        )

    def half_copy(h, k):
        px, py = plane_peer(k)
        columns = pl.ds(h * HALF, HALF)
        return pltpu.make_async_remote_copy(
            src_ref=plane_out.at[0, block16(px * 4 + py), columns],
            dst_ref=plane_in.at[0, block16(mine), columns],
            send_sem=p_send.at[4 * h, k],
            recv_sem=p_recv.at[4 * h, k],
            device_id=device(px, py, z, c),
            device_id_type=MESH,
        )

    def half_start(h):
        @pl.loop(1, 16)
        def _(k):
            half_copy(h, k).start()

        columns = pl.ds(h * HALF, HALF)
        plane_in[0, block16(mine), columns] = plane_out[0, block16(mine), columns]

    def half_finish(h):
        @pl.loop(1, 16)
        def _(k):
            half_copy(h, k).wait_recv()

    def plane_start(a):
        @pl.loop(1, 16)
        def _(k):
            plane_copy(a, k).start()

        plane_in[a, block16(mine)] = plane_out[a, block16(mine)]

    def plane_finish(a):
        @pl.loop(1, 16)
        def _(k):
            plane_copy(a, k).wait_recv()

    def line_copy(a, j, columns=pl.ds(0, WIDTH)):
        q = (zh + (j >> 1)) & 3
        pc = c ^ (j & 1)
        k = (z - 2 * q + 11) & 7
        low = k >> 2
        far = jnp.where(low == 1, k - 4, 3 - k)
        return pltpu.make_async_remote_copy(
            src_ref=line_out.at[a, block32(q * 2 + pc), columns],
            dst_ref=rows.at[a, block32(k * 2 + c), columns],
            send_sem=l_send.at[a, j],
            recv_sem=l_recv.at[a, far * 2 + (j & 1)],
            device_id=device(x, y, 2 * q + low, pc),
            device_id_type=MESH,
        )

    def near_row(t, pc):
        return (3 + zl + side * t) * 2 + pc

    def own_copy(a, j, columns):
        pc = c ^ j
        return pltpu.make_async_remote_copy(
            src_ref=line_out.at[a, block32(zh * 2 + pc), columns],
            dst_ref=rows.at[a, block32((3 + zl) * 2 + c), columns],
            send_sem=f_send.at[a, j],
            recv_sem=f_recv.at[a, j],
            device_id=device(x, y, z ^ 1, pc),
            device_id_type=MESH,
        )

    def line_start(a, columns=pl.ds(0, WIDTH)):
        for dq in (1, 3):
            for dc in range(2):
                line_copy(a, 2 * dq + dc, columns).start()
        line_copy(a, 1, columns).start()
        for dc in range(2):
            own_copy(a, dc, columns).start()
        for dc in range(2):
            line_copy(a, 4 + dc, columns).start()
        rows[a, block32((3 + zl) * 2 + c), columns] = line_out[a, block32(zh * 2 + c), columns]

    def arrive(a, j):
        place = block32(near_row(j >> 1, c ^ (j & 1)))
        return pltpu.make_async_remote_copy(
            src_ref=rows.at[a, place],
            dst_ref=rows.at[a, place],
            send_sem=f_send.at[a, j],
            recv_sem=l_recv.at[a, j],
            device_id=twin,
            device_id_type=MESH,
        )

    def forward(a, j):
        place = block32(near_row(j >> 1, c ^ (j & 1)))
        return pltpu.make_async_remote_copy(
            src_ref=rows.at[a, place],
            dst_ref=rows.at[a, place],
            send_sem=f_send.at[a, j],
            recv_sem=f_recv.at[a, j],
            device_id=twin,
            device_id_type=MESH,
        )

    def pass_on(a, t):
        for dc in range(2):
            j = 2 * t + dc
            arrive(a, j).wait_recv()
            forward(a, j).start()

    def own_finish(a):
        arrive(a, 1).wait_recv()

    def far_finish(a):
        @pl.loop(0, 8)
        def _(j):
            forward(a, j).wait_recv()

    def near_chunk(low, t):
        return 3 - 3 * low + (2 * low - 1) * t

    def twin_copy(a, t):
        place = pl.ds(pl.multiple_of(near_chunk(1 - zl, t) * 64, 64), 64)
        return pltpu.make_async_remote_copy(
            src_ref=twin_out.at[a, place],
            dst_ref=twin_in.at[a, place],
            send_sem=c_send.at[a, t],
            recv_sem=c_recv.at[a, t],
            device_id=twin,
            device_id_type=MESH,
        )

    def back_copy(a, j):
        t = j >> 1
        pc = c ^ (j & 1)
        pz = (z + side * t + 8) & 7
        shift = (zh - (pz >> 1) + 4) & 3
        return pltpu.make_async_remote_copy(
            src_ref=line_out.at[2 + a, block32(near_row(t, pc) - 8 * zl)],
            dst_ref=line_in.at[a, block32(zh * 2 + c)],
            send_sem=l_send.at[2 + a, j],
            recv_sem=l_recv.at[2 + a, shift * 2 + (j & 1)],
            device_id=device(x, y, pz, pc),
            device_id_type=MESH,
        )

    near_rows = pl.ds(pl.multiple_of(zl * NEAR, NEAR), NEAR)
    far_rows = pl.ds(pl.multiple_of((1 - zl) * NEAR, NEAR), NEAR)

    def back_finish(a):
        @pl.loop(1, 8)
        def _(j):
            pltpu.make_async_remote_copy(
                src_ref=line_in.at[a, block32(0)],
                dst_ref=line_in.at[a, block32(0)],
                send_sem=l_send.at[2 + a, j],
                recv_sem=l_recv.at[2 + a, j],
                device_id=twin,
                device_id_type=MESH,
            ).wait_recv()

    swap[...] = one_hot(SLOTS, SLOTS, swap_slots)
    tok[TOKENS - 4 :, :] = jnp.zeros((PAD - TOKENS + 4, WIDTH), BF16)
    go[TOKENS - 4 :, :] = jnp.zeros((PAD - TOKENS + 4, WIDTH), BF16)
    for copy in i_copies:
        copy.wait()
    tok[0:TOKENS, :] = tok_ref[0]
    go[0:TOKENS, :] = go_ref[0]
    spp[...] = dot(sp_ref[...], swap[...]).astype(BF16)
    logits = dot(tok[...], spp[...])
    valid = lax.broadcasted_iota(jnp.int32, (PAD, SLOTS), 0) < TOKENS
    masked = jnp.where(valid, logits, -1e30)
    raised = jnp.exp(masked - jnp.max(masked, axis=0, keepdims=True))
    dispatch = raised / jnp.sum(raised, axis=0, keepdims=True)
    disp[...] = dispatch
    disp_b[...] = dispatch.astype(BF16)
    plane_out[0, :, 0:HALF] = dot(disp_b[...], tok[:, 0:HALF], 0, 0).astype(BF16)
    pl.semaphore_wait(barrier, 30)
    half_start(0)
    plane_out[0, :, HALF:WIDTH] = dot(disp_b[...], tok[:, HALF:WIDTH], 0, 0).astype(BF16)
    half_start(1)
    raised = jnp.exp(logits - jnp.max(logits, axis=1, keepdims=True))
    combine = raised / jnp.sum(raised, axis=1, keepdims=True)
    comb[...] = combine
    plane_out[1] = dot(combine.astype(BF16), go[...], 0, 0).astype(BF16)
    plane_start(1)
    line[...] = one_hot(SLOTS, SLOTS, to_line)
    for h in range(2):
        half_finish(h)
        columns = pl.ds(h * HALF, HALF)
        line_out[0, :, columns] = dot(line[...], plane_in[0, :, columns]).astype(BF16)
        line_start(0, columns)
    plane[...] = one_hot(SLOTS, SLOTS, to_plane)
    tok_t[...] = tok[...].T
    pass_on(0, 1)
    plane_finish(1)
    line_out[1] = dot(line[...], plane_in[1]).astype(BF16)
    line_start(1)
    pass_on(0, 2)
    pass_on(0, 3)
    own_finish(0)
    for copy in w_copies:
        copy.wait()

    def activate(place):
        @pl.loop(0, HALF_HIDDEN // TILE)
        def _(j):
            tile = pl.ds(pl.multiple_of(j * TILE, TILE), TILE)
            pre = dot(rows[0, place], win[:, tile])
            square = pre * pre
            tanh = jnp.tanh(ROOT * pre * (1.0 + 0.044715 * square))
            half = 0.5 * (1.0 + tanh)
            act[place, tile] = (pre * half).astype(BF16)
            slope[place, tile] = half + (0.5 * ROOT) * pre * (1.0 - tanh * tanh) * (
                1.0 + (3 * 0.044715) * square
            )

    def twin_rows(wide, weight, weight_dim, place, target, cast):
        @pl.loop(0, WIDTH // TILE)
        def _(j):
            tile = pl.ds(pl.multiple_of(j * TILE, TILE), TILE)
            if weight_dim == 0:
                value = dot(wide[place], weight[:, tile])
            else:
                value = dot(wide[place], weight[tile, :], 1, 1)
            target[:, tile] = value.astype(cast)

    def sum_back(a, t):
        twin_copy(a, t).wait_recv()
        place = pl.ds(pl.multiple_of(near_chunk(zl, t) * 64, 64), 64)
        line_out[2 + a, place] = (own[a, place] + twin_in[a, place].astype(F32)).astype(BF16)
        back_copy(a, 2 * t + 1).start()
        if t > 0:
            back_copy(a, 2 * t).start()
        else:
            line_in[a, block32(zh * 2 + c)] = line_out[2 + a, block32(near_row(0, c) - 8 * zl)]

    activate(near_rows)
    pass_on(1, 1)
    pass_on(1, 2)
    pass_on(1, 3)
    own_finish(1)
    far_finish(0)
    activate(far_rows)
    twin_rows(act, wout, 0, far_rows, twin_out.at[0], BF16)
    for t in (3, 2, 1, 0):
        twin_copy(0, t).start()
    twin_rows(act, wout, 0, near_rows, own.at[0], F32)
    far_finish(1)

    @pl.loop(0, HALF_HIDDEN // TILE)
    def _(j):
        tile = pl.ds(pl.multiple_of(j * TILE, TILE), TILE)
        gpre[:, tile] = (dot(rows[1], wout[tile, :], 1, 1) * slope[:, tile]).astype(BF16)

    twin_rows(gpre, win, 1, far_rows, twin_out.at[1], BF16)
    for t in (3, 2, 1, 0):
        sum_back(0, t)
        twin_copy(1, t).start()
    twin_rows(gpre, win, 1, near_rows, own.at[1], F32)

    def out_copies(j):
        tile = pl.ds(pl.multiple_of(j * TILE, TILE), TILE)
        return pltpu.make_async_copy(gwo.at[tile], gwo_hbm.at[0, tile], o_sem.at[0, j])

    def in_copies(j):
        tile = pl.ds(pl.multiple_of(j * TILE, TILE), TILE)
        return pltpu.make_async_copy(gwi.at[tile], gwi_hbm.at[0, tile], o_sem.at[1, j])

    @pl.loop(0, HALF_HIDDEN // TILE)
    def _(j):
        tile = pl.ds(pl.multiple_of(j * TILE, TILE), TILE)
        gwo[tile, :] = dot(act[:, tile], rows[1], 0, 0).astype(BF16)
        out_copies(j).start()

    sum_back(1, 3)
    sum_back(1, 2)
    back_finish(0)
    plane_out[2] = dot(plane[...], line_in[0]).astype(BF16)
    plane_start(2)
    sum_back(1, 1)
    sum_back(1, 0)
    plane_finish(2)
    gc = dot(go[...], plane_in[2], 1, 1)
    weight = comb[...]
    part = dot(
        (weight * (gc - jnp.sum(gc * weight, axis=1, keepdims=True))).astype(BF16), swap[...]
    ).astype(BF16)
    acc_t[...] = dot(part, sp_ref[...], 1, 1)
    grad_half = dot(tok_t[...], part)
    grad[0] = grad_half[:, 0:128]
    grad[1] = grad_half[:, 128:256]

    @pl.loop(0, WIDTH // TILE)
    def _(j):
        tile = pl.ds(pl.multiple_of(j * TILE, TILE), TILE)
        gwi[tile, :] = dot(rows[0, :, tile], gpre[...], 0, 0).astype(BF16)
        in_copies(j).start()

    back_finish(1)
    plane_out[3] = dot(plane[...], line_in[1]).astype(BF16)
    plane_start(3)
    plane_finish(3)
    gd = dot(tok[...], plane_in[3], 1, 1)
    weight = disp[...]
    part = dot(
        (weight * (gd - jnp.sum(gd * weight, axis=0, keepdims=True))).astype(BF16), swap[...]
    ).astype(BF16)
    part_s[...] = part

    def half(index):
        return pl.ds(pl.multiple_of(index * 128, 128), 128)

    other = dot(tok_t[...], part_s[:, half(c ^ 1)])
    core_out[...] = (grad[c ^ 1] + other).astype(BF16)
    core_copy = pltpu.make_async_remote_copy(
        src_ref=core_out,
        dst_ref=core_in,
        send_sem=g_send.at[0],
        recv_sem=g_recv.at[0],
        device_id=sibling,
        device_id_type=MESH,
    )
    core_copy.start()
    grad[c] += dot(tok_t[...], part_s[:, half(c)])
    core_copy.wait_recv()
    ar_out[...] = (grad[c] + core_in[...].astype(F32)).astype(BF16)

    def block48(index):
        return pl.ds(pl.multiple_of(index * 48, 48), 48)

    def reduce_copy(k):
        px, py = plane_peer(k)
        return pltpu.make_async_remote_copy(
            src_ref=ar_out.at[block48(px * 4 + py)],
            dst_ref=ar_in.at[block48(mine)],
            send_sem=a_send.at[0, k],
            recv_sem=a_recv.at[0, k],
            device_id=device(px, py, z, c),
            device_id_type=MESH,
        )

    @pl.loop(1, 16)
    def _(k):
        reduce_copy(k).start()

    ar_in[block48(mine)] = ar_out[block48(mine)]
    total = acc_t[...] + dot(part, sp_ref[...], 1, 1) + dot(disp_b[...], plane_in[3])
    for column in range(WIDTH // 128):
        gt[pl.ds(column, TOKENS, stride=WIDTH // 128), :] = total[
            0:TOKENS, 128 * column : 128 * column + 128
        ]
    gt_copy = pltpu.make_async_copy(gt, gt_hbm, o_sem.at[0, 6])
    gt_copy.start()

    @pl.loop(1, 16)
    def _(k):
        reduce_copy(k).wait_recv()

    plane_sum = ar_in[0:48].astype(F32)
    for k in range(1, 16):
        plane_sum += ar_in[48 * k : 48 * k + 48].astype(F32)
    z_out[...] = plane_sum.astype(BF16)

    def z_copy(k):
        return pltpu.make_async_remote_copy(
            src_ref=z_out,
            dst_ref=z_in.at[z],
            send_sem=z_send.at[k],
            recv_sem=z_recv.at[k],
            device_id=device(x, y, (z + k) & 7, c),
            device_id_type=MESH,
        )

    @pl.loop(1, 8)
    def _(k):
        z_copy(k).start()

    z_in[z] = z_out[...]

    @pl.loop(1, 16)
    def _(k):
        for h in range(2):
            half_copy(h, k).wait_send()
        for a in range(1, 4):
            plane_copy(a, k).wait_send()

    @pl.loop(1, 8)
    def _(k):
        for a in range(2):
            line_copy(a, k).wait_send()
            back_copy(a, k).wait_send()

    @pl.loop(0, 8)
    def _(k):
        for a in range(2):
            forward(a, k).wait_send()

    @pl.loop(0, 4)
    def _(t):
        for a in range(2):
            twin_copy(a, t).wait_send()

    core_copy.wait_send()

    @pl.loop(1, 8)
    def _(k):
        z_copy(k).wait_recv()

    line_sum = z_in[0].astype(F32)
    for k in range(1, 8):
        line_sum += z_in[k].astype(F32)
    done[c, block48(mine)] = line_sum.astype(BF16)

    def gather_copy(k):
        px, py = plane_peer(k)
        return pltpu.make_async_remote_copy(
            src_ref=done.at[c, block48(mine)],
            dst_ref=done.at[c, block48(mine)],
            send_sem=a_send.at[1, k],
            recv_sem=a_recv.at[1, k],
            device_id=device(px, py, z, c),
            device_id_type=MESH,
        )

    @pl.loop(1, 16)
    def _(k):
        gather_copy(k).start()

    @pl.loop(1, 16)
    def _(k):
        reduce_copy(k).wait_send()

    @pl.loop(1, 8)
    def _(k):
        z_copy(k).wait_send()

    @pl.loop(0, HALF_HIDDEN // TILE)
    def _(j):
        out_copies(j).wait()

    @pl.loop(0, WIDTH // TILE)
    def _(j):
        in_copies(j).wait()

    gt_copy.wait()

    @pl.loop(1, 16)
    def _(k):
        gather_copy(k).wait_recv()

    last_copy = pltpu.make_async_remote_copy(
        src_ref=done.at[c],
        dst_ref=done.at[c],
        send_sem=g_send.at[1],
        recv_sem=g_recv.at[1],
        device_id=sibling,
        device_id_type=MESH,
    )
    last_copy.start()

    gsp[:, half(c)] = done[c]

    @pl.loop(1, 16)
    def _(k):
        gather_copy(k).wait_send()

    last_copy.wait()
    gsp[:, half(c ^ 1)] = done[c ^ 1]
    gsp_copy = pltpu.make_async_copy(gsp, gsp_hbm, o_sem.at[0, 7])
    gsp_copy.start()
    gsp_copy.wait()


def body(tokens, grad_out, slot_param, weight_in, weight_out):
    flat = (tokens.shape[1] * tokens.shape[2] // 128, 128)
    hbm = pl.BlockSpec(memory_space=pl.ANY)
    dma = pltpu.SemaphoreType.DMA
    buffers = [
        (tokens.shape, BF16),
        (tokens.shape, BF16),
        (slot_param.shape, BF16),
        ((SLOTS, SLOTS), BF16),
        ((SLOTS, SLOTS), BF16),
        ((SLOTS, SLOTS), BF16),
        ((PAD, SLOTS), BF16),
        (flat, F32),
        (slot_param.shape, BF16),
        ((PAD, WIDTH), BF16),
        ((PAD, WIDTH), BF16),
        ((WIDTH, PAD), BF16),
        ((WIDTH, SLOTS), BF16),
        ((PAD, SLOTS), F32),
        ((PAD, SLOTS), F32),
        ((PAD, SLOTS), BF16),
        ((WIDTH, HALF_HIDDEN), BF16),
        ((HALF_HIDDEN, WIDTH), BF16),
        ((4, SLOTS, WIDTH), BF16),
        ((4, SLOTS, WIDTH), BF16),
        ((4, SLOTS, WIDTH), BF16),
        ((2, SLOTS, WIDTH), BF16),
        ((2, ROWS, WIDTH), BF16),
        ((2, NEAR, WIDTH), BF16),
        ((2, NEAR, WIDTH), BF16),
        ((2, NEAR, WIDTH), F32),
        ((ROWS, HALF_HIDDEN), BF16),
        ((ROWS, HALF_HIDDEN), F32),
        ((ROWS, HALF_HIDDEN), BF16),
        ((WIDTH, HALF_HIDDEN), BF16),
        ((HALF_HIDDEN, WIDTH), BF16),
        ((PAD, WIDTH), F32),
        ((2, WIDTH, 128), F32),
        ((WIDTH, 128), BF16),
        ((WIDTH, 128), BF16),
        ((WIDTH, 128), BF16),
        ((WIDTH, 128), BF16),
        ((48, 128), BF16),
        ((8, 48, 128), BF16),
        ((2, WIDTH, 128), BF16),
    ]
    grad_tokens, grad_in, grad_out, grad_slots = pl.pallas_call(
        kernel,
        out_shape=(
            jax.ShapeDtypeStruct(flat, F32),
            jax.ShapeDtypeStruct(weight_in.shape, BF16),
            jax.ShapeDtypeStruct(weight_out.shape, BF16),
            jax.ShapeDtypeStruct(slot_param.shape, BF16),
        ),
        in_specs=[pl.BlockSpec(memory_space=pltpu.HBM)] * 5,
        out_specs=(hbm,) * 4,
        scratch_shapes=[pltpu.VMEM(shape, kind) for shape, kind in buffers]
        + [
            dma((5,)),
            dma((2, 8)),
            dma((5, 16)),
            dma((5, 16)),
            dma((4, 8)),
            dma((4, 8)),
            dma((2, 8)),
            dma((2, 8)),
            dma((2, 4)),
            dma((2, 4)),
            dma((2, 16)),
            dma((2, 16)),
            dma((2,)),
            dma((2,)),
            dma((8,)),
            dma((8,)),
        ],
        compiler_params=pltpu.CompilerParams(
            collective_id=0, has_side_effects=True, vmem_limit_bytes=46 * 1024 * 1024
        ),
    )(tokens, grad_out, slot_param, weight_in, weight_out)
    return grad_tokens.reshape(tokens.shape), grad_in, grad_out, grad_slots.astype(F32)


def solution(mesh):
    return jax.shard_map(
        body,
        mesh=mesh,
        in_specs=(
            P(("expert", "hid"), None, None),
            P(("expert", "hid"), None, None),
            P(),
            P("expert", None, "hid"),
            P("expert", "hid", None),
        ),
        out_specs=(
            P(("expert", "hid"), None, None),
            P("expert", None, "hid"),
            P("expert", "hid", None),
            P(),
        ),
        check_vma=False,
    )
```

```python
import math

import jax
import jax.numpy as jnp
from jax import lax
from jax.experimental import pallas as pl
from jax.experimental.pallas import tpu as pltpu
from jax.sharding import PartitionSpec as P

F32 = jnp.float32
BF16 = jnp.bfloat16
MESH = pl.DeviceIdType.MESH

TOKENS = 196
PAD = 208
WIDTH = 768
HALF_HIDDEN = 1536
SLOTS = 256
ROWS = 512
NEAR = 256
BLOCK = 32
HALF = 384
TILE = 256
ROOT = math.sqrt(2.0 / math.pi)


def dot(left, right, left_dim=1, right_dim=0):
    return lax.dot_general(
        left, right, (((left_dim,), (right_dim,)), ((), ())), preferred_element_type=F32
    )


def one_hot(rows, columns, source):
    row = lax.broadcasted_iota(jnp.int32, (rows, columns), 0)
    column = lax.broadcasted_iota(jnp.int32, (rows, columns), 1)
    return jnp.where(source(row) == column, 1.0, 0.0).astype(BF16)


def swap_slots(index):
    return (index & 0xC3) | ((index & 0x30) >> 2) | ((index & 0x0C) << 2)


def to_line(index):
    return (((index >> 1) & 15) << 4) | ((index >> 5) << 1) | (index & 1)


def to_plane(index):
    return (((index >> 1) & 7) << 5) | ((index >> 4) << 1) | (index & 1)


def kernel(
    tok_hbm,
    go_hbm,
    sp_hbm,
    win_hbm,
    wout_hbm,
    gt_hbm,
    gwi_hbm,
    gwo_hbm,
    gsp_hbm,
    tok_ref,
    go_ref,
    sp_ref,
    line,
    plane,
    swap,
    part_s,
    gt,
    gsp,
    tok,
    go,
    tok_t,
    spp,
    disp,
    comb,
    disp_b,
    win,
    wout,
    plane_out,
    plane_in,
    line_out,
    line_in,
    rows,
    twin_out,
    twin_in,
    own,
    act,
    slope,
    gpre,
    gwi,
    gwo,
    acc_t,
    grad,
    core_out,
    core_in,
    ar_out,
    ar_in,
    z_out,
    z_in,
    done,
    w_sem,
    o_sem,
    p_send,
    p_recv,
    l_send,
    l_recv,
    f_send,
    f_recv,
    c_send,
    c_recv,
    a_send,
    a_recv,
    g_send,
    g_recv,
    z_send,
    z_recv,
):
    expert = lax.axis_index("expert")
    zl = lax.axis_index("hid")
    x = expert >> 5
    zh = (expert >> 3) & 3
    y = (expert >> 1) & 3
    c = expert & 1
    z = zh * 2 + zl
    mine = x * 4 + y
    side = 2 * zl - 1

    def device(px, py, pz, pc):
        return {
            "expert": (((px * 4 + (pz >> 1)) * 4 + py) * 2) + pc,
            "hid": pz & 1,
        }

    twin = device(x, y, z ^ 1, c)
    sibling = device(x, y, z, c ^ 1)

    def plane_peer(k):
        return (x + (k >> 2)) & 3, (y + (k & 3)) & 3

    i_copies = [
        pltpu.make_async_copy(sp_hbm, sp_ref, w_sem.at[2]),
        pltpu.make_async_copy(tok_hbm, tok_ref, w_sem.at[3]),
        pltpu.make_async_copy(go_hbm, go_ref, w_sem.at[4]),
    ]
    w_copies = [
        pltpu.make_async_copy(win_hbm.at[0], win, w_sem.at[0]),
        pltpu.make_async_copy(wout_hbm.at[0], wout, w_sem.at[1]),
    ]
    for copy in i_copies + w_copies:
        copy.start()

    barrier = pltpu.get_barrier_semaphore()

    @pl.loop(1, 16)
    def _(k):
        px, py = plane_peer(k)
        pl.semaphore_signal(barrier, inc=1, device_id=device(px, py, z, c), device_id_type=MESH)
        pl.semaphore_signal(
            barrier,
            inc=1,
            device_id=device(x, y, (z + (k >> 1)) & 7, c ^ (k & 1)),
            device_id_type=MESH,
        )

    def block16(index):
        return pl.ds(pl.multiple_of(index * 16, 16), 16)

    def block32(index):
        return pl.ds(pl.multiple_of(index * BLOCK, BLOCK), BLOCK)

    def plane_copy(a, k):
        px, py = plane_peer(k)
        return pltpu.make_async_remote_copy(
            src_ref=plane_out.at[a, block16(px * 4 + py)],
            dst_ref=plane_in.at[a, block16(mine)],
            send_sem=p_send.at[a, k],
            recv_sem=p_recv.at[a, k],
            device_id=device(px, py, z, c),
            device_id_type=MESH,
        )

    def half_copy(h, k):
        px, py = plane_peer(k)
        columns = pl.ds(h * HALF, HALF)
        return pltpu.make_async_remote_copy(
            src_ref=plane_out.at[0, block16(px * 4 + py), columns],
            dst_ref=plane_in.at[0, block16(mine), columns],
            send_sem=p_send.at[4 * h, k],
            recv_sem=p_recv.at[4 * h, k],
            device_id=device(px, py, z, c),
            device_id_type=MESH,
        )

    def half_start(h):
        @pl.loop(1, 16)
        def _(k):
            half_copy(h, k).start()

        columns = pl.ds(h * HALF, HALF)
        plane_in[0, block16(mine), columns] = plane_out[0, block16(mine), columns]

    def half_finish(h):
        @pl.loop(1, 16)
        def _(k):
            half_copy(h, k).wait_recv()

    def plane_start(a):
        @pl.loop(1, 16)
        def _(k):
            plane_copy(a, k).start()

        plane_in[a, block16(mine)] = plane_out[a, block16(mine)]

    def plane_finish(a):
        @pl.loop(1, 16)
        def _(k):
            plane_copy(a, k).wait_recv()

    def line_copy(a, j, columns=pl.ds(0, WIDTH)):
        q = (zh + (j >> 1)) & 3
        pc = c ^ (j & 1)
        k = (z - 2 * q + 11) & 7
        low = k >> 2
        far = jnp.where(low == 1, k - 4, 3 - k)
        return pltpu.make_async_remote_copy(
            src_ref=line_out.at[a, block32(q * 2 + pc), columns],
            dst_ref=rows.at[a, block32(k * 2 + c), columns],
            send_sem=l_send.at[a, j],
            recv_sem=l_recv.at[a, far * 2 + (j & 1)],
            device_id=device(x, y, 2 * q + low, pc),
            device_id_type=MESH,
        )

    def near_row(t, pc):
        return (3 + zl + side * t) * 2 + pc

    def own_copy(a, j, columns):
        pc = c ^ j
        return pltpu.make_async_remote_copy(
            src_ref=line_out.at[a, block32(zh * 2 + pc), columns],
            dst_ref=rows.at[a, block32((3 + zl) * 2 + c), columns],
            send_sem=f_send.at[a, j],
            recv_sem=f_recv.at[a, j],
            device_id=device(x, y, z ^ 1, pc),
            device_id_type=MESH,
        )

    def line_start(a, columns=pl.ds(0, WIDTH)):
        for dq in (1, 3):
            for dc in range(2):
                line_copy(a, 2 * dq + dc, columns).start()
        line_copy(a, 1, columns).start()
        for dc in range(2):
            own_copy(a, dc, columns).start()
        for dc in range(2):
            line_copy(a, 4 + dc, columns).start()
        rows[a, block32((3 + zl) * 2 + c), columns] = line_out[a, block32(zh * 2 + c), columns]

    def arrive(a, j):
        place = block32(near_row(j >> 1, c ^ (j & 1)))
        return pltpu.make_async_remote_copy(
            src_ref=rows.at[a, place],
            dst_ref=rows.at[a, place],
            send_sem=f_send.at[a, j],
            recv_sem=l_recv.at[a, j],
            device_id=twin,
            device_id_type=MESH,
        )

    def forward(a, j):
        place = block32(near_row(j >> 1, c ^ (j & 1)))
        return pltpu.make_async_remote_copy(
            src_ref=rows.at[a, place],
            dst_ref=rows.at[a, place],
            send_sem=f_send.at[a, j],
            recv_sem=f_recv.at[a, j],
            device_id=twin,
            device_id_type=MESH,
        )

    def pass_on(a, t):
        for dc in range(2):
            j = 2 * t + dc
            arrive(a, j).wait_recv()
            forward(a, j).start()

    def own_finish(a):
        arrive(a, 1).wait_recv()

    def far_finish(a):
        @pl.loop(0, 8)
        def _(j):
            forward(a, j).wait_recv()

    def near_chunk(low, t):
        return 3 - 3 * low + (2 * low - 1) * t

    def twin_copy(a, t):
        place = pl.ds(pl.multiple_of(near_chunk(1 - zl, t) * 64, 64), 64)
        return pltpu.make_async_remote_copy(
            src_ref=twin_out.at[a, place],
            dst_ref=twin_in.at[a, place],
            send_sem=c_send.at[a, t],
            recv_sem=c_recv.at[a, t],
            device_id=twin,
            device_id_type=MESH,
        )

    def back_copy(a, j):
        t = j >> 1
        pc = c ^ (j & 1)
        pz = (z + side * t + 8) & 7
        shift = (zh - (pz >> 1) + 4) & 3
        return pltpu.make_async_remote_copy(
            src_ref=line_out.at[2 + a, block32(near_row(t, pc) - 8 * zl)],
            dst_ref=line_in.at[a, block32(zh * 2 + c)],
            send_sem=l_send.at[2 + a, j],
            recv_sem=l_recv.at[2 + a, shift * 2 + (j & 1)],
            device_id=device(x, y, pz, pc),
            device_id_type=MESH,
        )

    near_rows = pl.ds(pl.multiple_of(zl * NEAR, NEAR), NEAR)
    far_rows = pl.ds(pl.multiple_of((1 - zl) * NEAR, NEAR), NEAR)

    def back_finish(a):
        @pl.loop(1, 8)
        def _(j):
            pltpu.make_async_remote_copy(
                src_ref=line_in.at[a, block32(0)],
                dst_ref=line_in.at[a, block32(0)],
                send_sem=l_send.at[2 + a, j],
                recv_sem=l_recv.at[2 + a, j],
                device_id=twin,
                device_id_type=MESH,
            ).wait_recv()

    swap[...] = one_hot(SLOTS, SLOTS, swap_slots)
    tok[TOKENS - 4 :, :] = jnp.zeros((PAD - TOKENS + 4, WIDTH), BF16)
    go[TOKENS - 4 :, :] = jnp.zeros((PAD - TOKENS + 4, WIDTH), BF16)
    for copy in i_copies:
        copy.wait()
    tok[0:TOKENS, :] = tok_ref[0]
    go[0:TOKENS, :] = go_ref[0]
    spp[...] = dot(sp_ref[...], swap[...]).astype(BF16)
    logits = dot(tok[...], spp[...])
    valid = lax.broadcasted_iota(jnp.int32, (PAD, SLOTS), 0) < TOKENS
    masked = jnp.where(valid, logits, -1e30)
    raised = jnp.exp(masked - jnp.max(masked, axis=0, keepdims=True))
    dispatch = raised / jnp.sum(raised, axis=0, keepdims=True)
    disp[...] = dispatch
    disp_b[...] = dispatch.astype(BF16)
    plane_out[0, :, 0:HALF] = dot(disp_b[...], tok[:, 0:HALF], 0, 0).astype(BF16)
    pl.semaphore_wait(barrier, 30)
    half_start(0)
    plane_out[0, :, HALF:WIDTH] = dot(disp_b[...], tok[:, HALF:WIDTH], 0, 0).astype(BF16)
    half_start(1)
    raised = jnp.exp(logits - jnp.max(logits, axis=1, keepdims=True))
    combine = raised / jnp.sum(raised, axis=1, keepdims=True)
    comb[...] = combine
    plane_out[1] = dot(combine.astype(BF16), go[...], 0, 0).astype(BF16)
    plane_start(1)
    line[...] = one_hot(SLOTS, SLOTS, to_line)
    for h in range(2):
        half_finish(h)
        columns = pl.ds(h * HALF, HALF)
        line_out[0, :, columns] = dot(line[...], plane_in[0, :, columns]).astype(BF16)
        line_start(0, columns)
    plane[...] = one_hot(SLOTS, SLOTS, to_plane)
    tok_t[...] = tok[...].T
    pass_on(0, 1)
    plane_finish(1)
    line_out[1] = dot(line[...], plane_in[1]).astype(BF16)
    line_start(1)
    pass_on(0, 2)
    pass_on(0, 3)
    own_finish(0)
    for copy in w_copies:
        copy.wait()

    def activate(place):
        @pl.loop(0, HALF_HIDDEN // TILE)
        def _(j):
            tile = pl.ds(pl.multiple_of(j * TILE, TILE), TILE)
            pre = dot(rows[0, place], win[:, tile])
            square = pre * pre
            tanh = jnp.tanh(ROOT * pre * (1.0 + 0.044715 * square))
            half = 0.5 * (1.0 + tanh)
            act[place, tile] = (pre * half).astype(BF16)
            slope[place, tile] = half + (0.5 * ROOT) * pre * (1.0 - tanh * tanh) * (
                1.0 + (3 * 0.044715) * square
            )

    def twin_rows(wide, weight, weight_dim, place, target, cast):
        @pl.loop(0, WIDTH // TILE)
        def _(j):
            tile = pl.ds(pl.multiple_of(j * TILE, TILE), TILE)
            if weight_dim == 0:
                value = dot(wide[place], weight[:, tile])
            else:
                value = dot(wide[place], weight[tile, :], 1, 1)
            target[:, tile] = value.astype(cast)

    def sum_back(a, t):
        twin_copy(a, t).wait_recv()
        place = pl.ds(pl.multiple_of(near_chunk(zl, t) * 64, 64), 64)
        line_out[2 + a, place] = (own[a, place] + twin_in[a, place].astype(F32)).astype(BF16)
        back_copy(a, 2 * t + 1).start()
        if t > 0:
            back_copy(a, 2 * t).start()
        else:
            line_in[a, block32(zh * 2 + c)] = line_out[2 + a, block32(near_row(0, c) - 8 * zl)]

    activate(near_rows)
    pass_on(1, 1)
    pass_on(1, 2)
    pass_on(1, 3)
    own_finish(1)
    far_finish(0)
    activate(far_rows)
    twin_rows(act, wout, 0, far_rows, twin_out.at[0], BF16)
    for t in (3, 2, 1, 0):
        twin_copy(0, t).start()
    twin_rows(act, wout, 0, near_rows, own.at[0], F32)
    far_finish(1)

    @pl.loop(0, HALF_HIDDEN // TILE)
    def _(j):
        tile = pl.ds(pl.multiple_of(j * TILE, TILE), TILE)
        gpre[:, tile] = (dot(rows[1], wout[tile, :], 1, 1) * slope[:, tile]).astype(BF16)

    twin_rows(gpre, win, 1, far_rows, twin_out.at[1], BF16)
    for t in (3, 2, 1, 0):
        sum_back(0, t)
        twin_copy(1, t).start()
    twin_rows(gpre, win, 1, near_rows, own.at[1], F32)

    def out_copies(j):
        tile = pl.ds(pl.multiple_of(j * TILE, TILE), TILE)
        return pltpu.make_async_copy(gwo.at[tile], gwo_hbm.at[0, tile], o_sem.at[0, j])

    def in_copies(j):
        tile = pl.ds(pl.multiple_of(j * TILE, TILE), TILE)
        return pltpu.make_async_copy(gwi.at[tile], gwi_hbm.at[0, tile], o_sem.at[1, j])

    sum_back(1, 3)
    sum_back(1, 2)
    back_finish(0)
    plane_out[2] = dot(plane[...], line_in[0]).astype(BF16)
    plane_start(2)
    sum_back(1, 1)
    sum_back(1, 0)
    plane_finish(2)
    gc = dot(go[...], plane_in[2], 1, 1)
    weight = comb[...]
    part = dot(
        (weight * (gc - jnp.sum(gc * weight, axis=1, keepdims=True))).astype(BF16), swap[...]
    ).astype(BF16)
    acc_t[...] = dot(part, sp_ref[...], 1, 1)
    grad_half = dot(tok_t[...], part)
    grad[0] = grad_half[:, 0:128]
    grad[1] = grad_half[:, 128:256]

    back_finish(1)
    plane_out[3] = dot(plane[...], line_in[1]).astype(BF16)
    plane_start(3)

    @pl.loop(0, HALF_HIDDEN // TILE)
    def _(j):
        tile = pl.ds(pl.multiple_of(j * TILE, TILE), TILE)
        gwo[tile, :] = dot(act[:, tile], rows[1], 0, 0).astype(BF16)
        out_copies(j).start()

    @pl.loop(0, WIDTH // TILE)
    def _(j):
        tile = pl.ds(pl.multiple_of(j * TILE, TILE), TILE)
        gwi[tile, :] = dot(rows[0, :, tile], gpre[...], 0, 0).astype(BF16)
        in_copies(j).start()

    plane_finish(3)
    gd = dot(tok[...], plane_in[3], 1, 1)
    weight = disp[...]
    part = dot(
        (weight * (gd - jnp.sum(gd * weight, axis=0, keepdims=True))).astype(BF16), swap[...]
    ).astype(BF16)
    part_s[...] = part

    def half(index):
        return pl.ds(pl.multiple_of(index * 128, 128), 128)

    other = dot(tok_t[...], part_s[:, half(c ^ 1)])
    core_out[...] = (grad[c ^ 1] + other).astype(BF16)
    core_copy = pltpu.make_async_remote_copy(
        src_ref=core_out,
        dst_ref=core_in,
        send_sem=g_send.at[0],
        recv_sem=g_recv.at[0],
        device_id=sibling,
        device_id_type=MESH,
    )
    core_copy.start()
    grad[c] += dot(tok_t[...], part_s[:, half(c)])
    core_copy.wait_recv()
    ar_out[...] = (grad[c] + core_in[...].astype(F32)).astype(BF16)

    def block48(index):
        return pl.ds(pl.multiple_of(index * 48, 48), 48)

    def reduce_copy(k):
        px, py = plane_peer(k)
        return pltpu.make_async_remote_copy(
            src_ref=ar_out.at[block48(px * 4 + py)],
            dst_ref=ar_in.at[block48(mine)],
            send_sem=a_send.at[0, k],
            recv_sem=a_recv.at[0, k],
            device_id=device(px, py, z, c),
            device_id_type=MESH,
        )

    @pl.loop(1, 16)
    def _(k):
        reduce_copy(k).start()

    ar_in[block48(mine)] = ar_out[block48(mine)]
    total = acc_t[...] + dot(part, sp_ref[...], 1, 1) + dot(disp_b[...], plane_in[3])
    for column in range(WIDTH // 128):
        gt[pl.ds(column, TOKENS, stride=WIDTH // 128), :] = total[
            0:TOKENS, 128 * column : 128 * column + 128
        ]
    gt_copy = pltpu.make_async_copy(gt, gt_hbm, o_sem.at[0, 6])
    gt_copy.start()

    @pl.loop(1, 16)
    def _(k):
        reduce_copy(k).wait_recv()

    plane_sum = ar_in[0:48].astype(F32)
    for k in range(1, 16):
        plane_sum += ar_in[48 * k : 48 * k + 48].astype(F32)
    z_out[...] = plane_sum.astype(BF16)

    def z_copy(k):
        return pltpu.make_async_remote_copy(
            src_ref=z_out,
            dst_ref=z_in.at[z],
            send_sem=z_send.at[k],
            recv_sem=z_recv.at[k],
            device_id=device(x, y, (z + k) & 7, c),
            device_id_type=MESH,
        )

    @pl.loop(1, 8)
    def _(k):
        z_copy(k).start()

    z_in[z] = z_out[...]

    @pl.loop(1, 16)
    def _(k):
        for h in range(2):
            half_copy(h, k).wait_send()
        for a in range(1, 4):
            plane_copy(a, k).wait_send()

    @pl.loop(1, 8)
    def _(k):
        for a in range(2):
            line_copy(a, k).wait_send()
            back_copy(a, k).wait_send()

    @pl.loop(0, 8)
    def _(k):
        for a in range(2):
            forward(a, k).wait_send()

    @pl.loop(0, 4)
    def _(t):
        for a in range(2):
            twin_copy(a, t).wait_send()

    core_copy.wait_send()

    @pl.loop(1, 8)
    def _(k):
        z_copy(k).wait_recv()

    line_sum = z_in[0].astype(F32)
    for k in range(1, 8):
        line_sum += z_in[k].astype(F32)
    done[c, block48(mine)] = line_sum.astype(BF16)

    def gather_copy(k):
        px, py = plane_peer(k)
        return pltpu.make_async_remote_copy(
            src_ref=done.at[c, block48(mine)],
            dst_ref=done.at[c, block48(mine)],
            send_sem=a_send.at[1, k],
            recv_sem=a_recv.at[1, k],
            device_id=device(px, py, z, c),
            device_id_type=MESH,
        )

    @pl.loop(1, 16)
    def _(k):
        gather_copy(k).start()

    @pl.loop(1, 16)
    def _(k):
        reduce_copy(k).wait_send()

    @pl.loop(1, 8)
    def _(k):
        z_copy(k).wait_send()

    @pl.loop(0, HALF_HIDDEN // TILE)
    def _(j):
        out_copies(j).wait()

    @pl.loop(0, WIDTH // TILE)
    def _(j):
        in_copies(j).wait()

    gt_copy.wait()

    @pl.loop(1, 16)
    def _(k):
        gather_copy(k).wait_recv()

    last_copy = pltpu.make_async_remote_copy(
        src_ref=done.at[c],
        dst_ref=done.at[c],
        send_sem=g_send.at[1],
        recv_sem=g_recv.at[1],
        device_id=sibling,
        device_id_type=MESH,
    )
    last_copy.start()

    gsp[:, half(c)] = done[c]

    @pl.loop(1, 16)
    def _(k):
        gather_copy(k).wait_send()

    last_copy.wait()
    gsp[:, half(c ^ 1)] = done[c ^ 1]
    gsp_copy = pltpu.make_async_copy(gsp, gsp_hbm, o_sem.at[0, 7])
    gsp_copy.start()
    gsp_copy.wait()


def body(tokens, grad_out, slot_param, weight_in, weight_out):
    arrays = (tokens, grad_out, slot_param, weight_in, weight_out)
    flat = (tokens.shape[1] * tokens.shape[2] // 128, 128)
    hbm = pl.BlockSpec(memory_space=pl.ANY)
    dma = pltpu.SemaphoreType.DMA
    buffers = [
        (tokens.shape, BF16),
        (tokens.shape, BF16),
        (slot_param.shape, BF16),
        ((SLOTS, SLOTS), BF16),
        ((SLOTS, SLOTS), BF16),
        ((SLOTS, SLOTS), BF16),
        ((PAD, SLOTS), BF16),
        (flat, F32),
        (slot_param.shape, BF16),
        ((PAD, WIDTH), BF16),
        ((PAD, WIDTH), BF16),
        ((WIDTH, PAD), BF16),
        ((WIDTH, SLOTS), BF16),
        ((PAD, SLOTS), F32),
        ((PAD, SLOTS), F32),
        ((PAD, SLOTS), BF16),
        ((WIDTH, HALF_HIDDEN), BF16),
        ((HALF_HIDDEN, WIDTH), BF16),
        ((4, SLOTS, WIDTH), BF16),
        ((4, SLOTS, WIDTH), BF16),
        ((4, SLOTS, WIDTH), BF16),
        ((2, SLOTS, WIDTH), BF16),
        ((2, ROWS, WIDTH), BF16),
        ((2, NEAR, WIDTH), BF16),
        ((2, NEAR, WIDTH), BF16),
        ((2, NEAR, WIDTH), F32),
        ((ROWS, HALF_HIDDEN), BF16),
        ((ROWS, HALF_HIDDEN), F32),
        ((ROWS, HALF_HIDDEN), BF16),
        ((WIDTH, HALF_HIDDEN), BF16),
        ((HALF_HIDDEN, WIDTH), BF16),
        ((PAD, WIDTH), F32),
        ((2, WIDTH, 128), F32),
        ((WIDTH, 128), BF16),
        ((WIDTH, 128), BF16),
        ((WIDTH, 128), BF16),
        ((WIDTH, 128), BF16),
        ((48, 128), BF16),
        ((8, 48, 128), BF16),
        ((2, WIDTH, 128), BF16),
    ]
    grad_tokens, grad_in, grad_out, grad_slots = pl.pallas_call(
        kernel,
        out_shape=(
            jax.ShapeDtypeStruct(flat, F32),
            jax.ShapeDtypeStruct(weight_in.shape, BF16),
            jax.ShapeDtypeStruct(weight_out.shape, BF16),
            jax.ShapeDtypeStruct(slot_param.shape, BF16),
        ),
        in_specs=[pl.BlockSpec(memory_space=pltpu.HBM)] * 5,
        out_specs=(hbm,) * 4,
        scratch_shapes=[pltpu.VMEM(shape, kind) for shape, kind in buffers]
        + [
            dma((5,)),
            dma((2, 8)),
            dma((5, 16)),
            dma((5, 16)),
            dma((4, 8)),
            dma((4, 8)),
            dma((2, 8)),
            dma((2, 8)),
            dma((2, 4)),
            dma((2, 4)),
            dma((2, 16)),
            dma((2, 16)),
            dma((2,)),
            dma((2,)),
            dma((8,)),
            dma((8,)),
        ],
        compiler_params=pltpu.CompilerParams(
            collective_id=0, has_side_effects=True, vmem_limit_bytes=46 * 1024 * 1024
        ),
    )(*(pltpu.with_memory_space_constraint(array, pltpu.HBM) for array in arrays))
    return grad_tokens.reshape(tokens.shape), grad_in, grad_out, grad_slots.astype(F32)


def solution(mesh):
    return jax.shard_map(
        body,
        mesh=mesh,
        in_specs=(
            P(("expert", "hid"), None, None),
            P(("expert", "hid"), None, None),
            P(),
            P("expert", None, "hid"),
            P("expert", "hid", None),
        ),
        out_specs=(
            P(("expert", "hid"), None, None),
            P("expert", None, "hid"),
            P("expert", "hid", None),
            P(),
        ),
        check_vma=False,
    )
```

```python
import math

import jax
import jax.numpy as jnp
from jax import lax
from jax.experimental import pallas as pl
from jax.experimental.pallas import tpu as pltpu
from jax.sharding import PartitionSpec as P

F32 = jnp.float32
BF16 = jnp.bfloat16
MESH = pl.DeviceIdType.MESH

TOKENS = 196
PAD = 208
WIDTH = 768
HALF_HIDDEN = 1536
SLOTS = 256
ROWS = 512
NEAR = 256
BLOCK = 32
HALF = 384
TILE = 256
ROOT = math.sqrt(2.0 / math.pi)


def dot(left, right, left_dim=1, right_dim=0):
    return lax.dot_general(
        left, right, (((left_dim,), (right_dim,)), ((), ())), preferred_element_type=F32
    )


def one_hot(rows, columns, source):
    row = lax.broadcasted_iota(jnp.int32, (rows, columns), 0)
    column = lax.broadcasted_iota(jnp.int32, (rows, columns), 1)
    return jnp.where(source(row) == column, 1.0, 0.0).astype(BF16)


def swap_slots(index):
    return (index & 0xC3) | ((index & 0x30) >> 2) | ((index & 0x0C) << 2)


def to_line(index):
    return (((index >> 1) & 15) << 4) | ((index >> 5) << 1) | (index & 1)


def to_plane(index):
    return (((index >> 1) & 7) << 5) | ((index >> 4) << 1) | (index & 1)


def kernel(
    tok_hbm,
    go_hbm,
    sp_hbm,
    win_hbm,
    wout_hbm,
    gt_hbm,
    gwi_hbm,
    gwo_hbm,
    gsp_hbm,
    tok_ref,
    go_ref,
    sp_ref,
    line,
    plane,
    swap,
    part_s,
    gt,
    tok,
    go,
    tok_t,
    spp,
    disp,
    comb,
    disp_b,
    win,
    wout,
    plane_out,
    plane_in,
    line_out,
    line_in,
    rows,
    twin_out,
    twin_in,
    own,
    act,
    slope,
    gpre,
    gwi,
    gwo,
    acc_t,
    grad,
    core_out,
    core_in,
    ar_out,
    ar_in,
    z_out,
    z_in,
    done,
    w_sem,
    o_sem,
    p_send,
    p_recv,
    l_send,
    l_recv,
    f_send,
    f_recv,
    c_send,
    c_recv,
    a_send,
    a_recv,
    g_send,
    g_recv,
    z_send,
    z_recv,
    g_result,
):
    expert = lax.axis_index("expert")
    zl = lax.axis_index("hid")
    x = expert >> 5
    zh = (expert >> 3) & 3
    y = (expert >> 1) & 3
    c = expert & 1
    z = zh * 2 + zl
    mine = x * 4 + y
    side = 2 * zl - 1

    def device(px, py, pz, pc):
        return {
            "expert": (((px * 4 + (pz >> 1)) * 4 + py) * 2) + pc,
            "hid": pz & 1,
        }

    twin = device(x, y, z ^ 1, c)
    sibling = device(x, y, z, c ^ 1)

    def plane_peer(k):
        return (x + (k >> 2)) & 3, (y + (k & 3)) & 3

    i_copies = [
        pltpu.make_async_copy(sp_hbm, sp_ref, w_sem.at[2]),
        pltpu.make_async_copy(tok_hbm, tok_ref, w_sem.at[3]),
        pltpu.make_async_copy(go_hbm, go_ref, w_sem.at[4]),
    ]
    w_copies = [
        pltpu.make_async_copy(win_hbm.at[0], win, w_sem.at[0]),
        pltpu.make_async_copy(wout_hbm.at[0], wout, w_sem.at[1]),
    ]
    for copy in i_copies + w_copies:
        copy.start()

    barrier = pltpu.get_barrier_semaphore()

    @pl.loop(1, 16)
    def _(k):
        px, py = plane_peer(k)
        pl.semaphore_signal(barrier, inc=1, device_id=device(px, py, z, c), device_id_type=MESH)
        pl.semaphore_signal(
            barrier,
            inc=1,
            device_id=device(x, y, (z + (k >> 1)) & 7, c ^ (k & 1)),
            device_id_type=MESH,
        )

    def block16(index):
        return pl.ds(pl.multiple_of(index * 16, 16), 16)

    def block32(index):
        return pl.ds(pl.multiple_of(index * BLOCK, BLOCK), BLOCK)

    def plane_copy(a, k):
        px, py = plane_peer(k)
        return pltpu.make_async_remote_copy(
            src_ref=plane_out.at[a, block16(px * 4 + py)],
            dst_ref=plane_in.at[a, block16(mine)],
            send_sem=p_send.at[a, k],
            recv_sem=p_recv.at[a, k],
            device_id=device(px, py, z, c),
            device_id_type=MESH,
        )

    def half_copy(h, k):
        px, py = plane_peer(k)
        columns = pl.ds(h * HALF, HALF)
        return pltpu.make_async_remote_copy(
            src_ref=plane_out.at[0, block16(px * 4 + py), columns],
            dst_ref=plane_in.at[0, block16(mine), columns],
            send_sem=p_send.at[4 * h, k],
            recv_sem=p_recv.at[4 * h, k],
            device_id=device(px, py, z, c),
            device_id_type=MESH,
        )

    def half_start(h):
        @pl.loop(1, 16)
        def _(k):
            half_copy(h, k).start()

        columns = pl.ds(h * HALF, HALF)
        plane_in[0, block16(mine), columns] = plane_out[0, block16(mine), columns]

    def half_finish(h):
        @pl.loop(1, 16)
        def _(k):
            half_copy(h, k).wait_recv()

    def plane_start(a):
        @pl.loop(1, 16)
        def _(k):
            plane_copy(a, k).start()

        plane_in[a, block16(mine)] = plane_out[a, block16(mine)]

    def plane_finish(a):
        @pl.loop(1, 16)
        def _(k):
            plane_copy(a, k).wait_recv()

    def line_copy(a, j, columns=pl.ds(0, WIDTH)):
        q = (zh + (j >> 1)) & 3
        pc = c ^ (j & 1)
        k = (z - 2 * q + 11) & 7
        low = k >> 2
        far = jnp.where(low == 1, k - 4, 3 - k)
        return pltpu.make_async_remote_copy(
            src_ref=line_out.at[a, block32(q * 2 + pc), columns],
            dst_ref=rows.at[a, block32(k * 2 + c), columns],
            send_sem=l_send.at[a, j],
            recv_sem=l_recv.at[a, far * 2 + (j & 1)],
            device_id=device(x, y, 2 * q + low, pc),
            device_id_type=MESH,
        )

    def near_row(t, pc):
        return (3 + zl + side * t) * 2 + pc

    def own_copy(a, j, columns):
        pc = c ^ j
        return pltpu.make_async_remote_copy(
            src_ref=line_out.at[a, block32(zh * 2 + pc), columns],
            dst_ref=rows.at[a, block32((3 + zl) * 2 + c), columns],
            send_sem=f_send.at[a, j],
            recv_sem=f_recv.at[a, j],
            device_id=device(x, y, z ^ 1, pc),
            device_id_type=MESH,
        )

    def line_start(a, columns=pl.ds(0, WIDTH)):
        for dq in (1, 3):
            for dc in range(2):
                line_copy(a, 2 * dq + dc, columns).start()
        line_copy(a, 1, columns).start()
        for dc in range(2):
            own_copy(a, dc, columns).start()
        for dc in range(2):
            line_copy(a, 4 + dc, columns).start()
        rows[a, block32((3 + zl) * 2 + c), columns] = line_out[a, block32(zh * 2 + c), columns]

    def arrive(a, j):
        place = block32(near_row(j >> 1, c ^ (j & 1)))
        return pltpu.make_async_remote_copy(
            src_ref=rows.at[a, place],
            dst_ref=rows.at[a, place],
            send_sem=f_send.at[a, j],
            recv_sem=l_recv.at[a, j],
            device_id=twin,
            device_id_type=MESH,
        )

    def forward(a, j):
        place = block32(near_row(j >> 1, c ^ (j & 1)))
        return pltpu.make_async_remote_copy(
            src_ref=rows.at[a, place],
            dst_ref=rows.at[a, place],
            send_sem=f_send.at[a, j],
            recv_sem=f_recv.at[a, j],
            device_id=twin,
            device_id_type=MESH,
        )

    def pass_on(a, t):
        for dc in range(2):
            j = 2 * t + dc
            arrive(a, j).wait_recv()
            forward(a, j).start()

    def own_finish(a):
        arrive(a, 1).wait_recv()

    def far_finish(a):
        @pl.loop(0, 8)
        def _(j):
            forward(a, j).wait_recv()

    def near_chunk(low, t):
        return 3 - 3 * low + (2 * low - 1) * t

    def twin_copy(a, t):
        place = pl.ds(pl.multiple_of(near_chunk(1 - zl, t) * 64, 64), 64)
        return pltpu.make_async_remote_copy(
            src_ref=twin_out.at[a, place],
            dst_ref=twin_in.at[a, place],
            send_sem=c_send.at[a, t],
            recv_sem=c_recv.at[a, t],
            device_id=twin,
            device_id_type=MESH,
        )

    def back_copy(a, j):
        t = j >> 1
        pc = c ^ (j & 1)
        pz = (z + side * t + 8) & 7
        shift = (zh - (pz >> 1) + 4) & 3
        return pltpu.make_async_remote_copy(
            src_ref=line_out.at[2 + a, block32(near_row(t, pc) - 8 * zl)],
            dst_ref=line_in.at[a, block32(zh * 2 + c)],
            send_sem=l_send.at[2 + a, j],
            recv_sem=l_recv.at[2 + a, shift * 2 + (j & 1)],
            device_id=device(x, y, pz, pc),
            device_id_type=MESH,
        )

    near_rows = pl.ds(pl.multiple_of(zl * NEAR, NEAR), NEAR)
    far_rows = pl.ds(pl.multiple_of((1 - zl) * NEAR, NEAR), NEAR)

    def back_finish(a):
        @pl.loop(1, 8)
        def _(j):
            pltpu.make_async_remote_copy(
                src_ref=line_in.at[a, block32(0)],
                dst_ref=line_in.at[a, block32(0)],
                send_sem=l_send.at[2 + a, j],
                recv_sem=l_recv.at[2 + a, j],
                device_id=twin,
                device_id_type=MESH,
            ).wait_recv()

    swap[...] = one_hot(SLOTS, SLOTS, swap_slots)
    tok[TOKENS - 4 :, :] = jnp.zeros((PAD - TOKENS + 4, WIDTH), BF16)
    go[TOKENS - 4 :, :] = jnp.zeros((PAD - TOKENS + 4, WIDTH), BF16)
    i_copies[0].wait()
    spp[...] = dot(sp_ref[...], swap[...]).astype(BF16)
    i_copies[1].wait()
    tok[0:TOKENS, :] = tok_ref[0]
    logits = dot(tok[...], spp[...])
    valid = lax.broadcasted_iota(jnp.int32, (PAD, SLOTS), 0) < TOKENS
    masked = jnp.where(valid, logits, -1e30)
    raised = jnp.exp(masked - jnp.max(masked, axis=0, keepdims=True))
    dispatch = raised / jnp.sum(raised, axis=0, keepdims=True)
    disp[...] = dispatch
    disp_b[...] = dispatch.astype(BF16)
    plane_out[0, :, 0:HALF] = dot(disp_b[...], tok[:, 0:HALF], 0, 0).astype(BF16)
    pl.semaphore_wait(barrier, 30)
    half_start(0)
    plane_out[0, :, HALF:WIDTH] = dot(disp_b[...], tok[:, HALF:WIDTH], 0, 0).astype(BF16)
    half_start(1)
    i_copies[2].wait()
    go[0:TOKENS, :] = go_ref[0]
    raised = jnp.exp(logits - jnp.max(logits, axis=1, keepdims=True))
    combine = raised / jnp.sum(raised, axis=1, keepdims=True)
    comb[...] = combine
    plane_out[1] = dot(combine.astype(BF16), go[...], 0, 0).astype(BF16)
    plane_start(1)
    line[...] = one_hot(SLOTS, SLOTS, to_line)
    for h in range(2):
        half_finish(h)
        columns = pl.ds(h * HALF, HALF)
        line_out[0, :, columns] = dot(line[...], plane_in[0, :, columns]).astype(BF16)
        line_start(0, columns)
    plane[...] = one_hot(SLOTS, SLOTS, to_plane)
    tok_t[...] = tok[...].T
    pass_on(0, 1)
    plane_finish(1)
    line_out[1] = dot(line[...], plane_in[1]).astype(BF16)
    line_start(1)
    pass_on(0, 2)
    pass_on(0, 3)
    own_finish(0)
    for copy in w_copies:
        copy.wait()

    def activate(place):
        @pl.loop(0, HALF_HIDDEN // TILE)
        def _(j):
            tile = pl.ds(pl.multiple_of(j * TILE, TILE), TILE)
            pre = dot(rows[0, place], win[:, tile])
            square = pre * pre
            tanh = jnp.tanh(ROOT * pre * (1.0 + 0.044715 * square))
            half = 0.5 * (1.0 + tanh)
            act[place, tile] = (pre * half).astype(BF16)
            slope[place, tile] = half + (0.5 * ROOT) * pre * (1.0 - tanh * tanh) * (
                1.0 + (3 * 0.044715) * square
            )

    def twin_rows(wide, weight, weight_dim, place, target, cast):
        @pl.loop(0, WIDTH // TILE)
        def _(j):
            tile = pl.ds(pl.multiple_of(j * TILE, TILE), TILE)
            if weight_dim == 0:
                value = dot(wide[place], weight[:, tile])
            else:
                value = dot(wide[place], weight[tile, :], 1, 1)
            target[:, tile] = value.astype(cast)

    def sum_back(a, t):
        twin_copy(a, t).wait_recv()
        place = pl.ds(pl.multiple_of(near_chunk(zl, t) * 64, 64), 64)
        line_out[2 + a, place] = (own[a, place] + twin_in[a, place].astype(F32)).astype(BF16)
        back_copy(a, 2 * t + 1).start()
        if t > 0:
            back_copy(a, 2 * t).start()
        else:
            line_in[a, block32(zh * 2 + c)] = line_out[2 + a, block32(near_row(0, c) - 8 * zl)]

    pass_on(1, 1)
    activate(near_rows)
    pass_on(1, 2)
    pass_on(1, 3)
    own_finish(1)
    far_finish(0)
    activate(far_rows)
    twin_rows(act, wout, 0, far_rows, twin_out.at[0], BF16)
    for t in (3, 2, 1, 0):
        twin_copy(0, t).start()
    twin_rows(act, wout, 0, near_rows, own.at[0], F32)

    def pull(place):
        @pl.loop(0, HALF_HIDDEN // TILE)
        def _(j):
            tile = pl.ds(pl.multiple_of(j * TILE, TILE), TILE)
            gpre[place, tile] = (dot(rows[1, place], wout[tile, :], 1, 1) * slope[place, tile]).astype(
                BF16
            )

    pull(near_rows)
    twin_rows(gpre, win, 1, near_rows, own.at[1], F32)
    far_finish(1)
    pull(far_rows)
    twin_rows(gpre, win, 1, far_rows, twin_out.at[1], BF16)
    for t in (3, 2, 1, 0):
        sum_back(0, t)
        twin_copy(1, t).start()

    def out_copies(j):
        tile = pl.ds(pl.multiple_of(j * TILE, TILE), TILE)
        return pltpu.make_async_copy(gwo.at[tile], gwo_hbm.at[0, tile], o_sem.at[0, j])

    def in_copies(j):
        tile = pl.ds(pl.multiple_of(j * TILE, TILE), TILE)
        return pltpu.make_async_copy(gwi.at[tile], gwi_hbm.at[0, tile], o_sem.at[1, j])

    sum_back(1, 3)
    sum_back(1, 2)
    back_finish(0)
    plane_out[2] = dot(plane[...], line_in[0]).astype(BF16)
    plane_start(2)
    sum_back(1, 1)
    sum_back(1, 0)
    plane_finish(2)
    gc = dot(go[...], plane_in[2], 1, 1)
    weight = comb[...]
    part = (weight * (gc - jnp.sum(gc * weight, axis=1, keepdims=True))).astype(BF16)
    acc_t[...] = dot(part, spp[...], 1, 1)
    grad_half = dot(tok_t[...], part)
    grad[0] = grad_half[:, 0:128]
    grad[1] = grad_half[:, 128:256]

    back_finish(1)
    plane_out[3] = dot(plane[...], line_in[1]).astype(BF16)
    plane_start(3)

    @pl.loop(0, HALF_HIDDEN // TILE)
    def _(j):
        tile = pl.ds(pl.multiple_of(j * TILE, TILE), TILE)
        gwo[tile, :] = dot(act[:, tile], rows[1], 0, 0).astype(BF16)
        out_copies(j).start()

    @pl.loop(0, WIDTH // TILE)
    def _(j):
        tile = pl.ds(pl.multiple_of(j * TILE, TILE), TILE)
        gwi[tile, :] = dot(rows[0, :, tile], gpre[...], 0, 0).astype(BF16)
        in_copies(j).start()

    plane_finish(3)
    gd = dot(tok[...], plane_in[3], 1, 1)
    weight = disp[...]
    part = (weight * (gd - jnp.sum(gd * weight, axis=0, keepdims=True))).astype(BF16)
    part_s[...] = part

    def half(index):
        return pl.ds(pl.multiple_of(index * 128, 128), 128)

    other = dot(tok_t[...], part_s[:, half(c ^ 1)])
    core_out[...] = (grad[c ^ 1] + other).astype(BF16)
    core_copy = pltpu.make_async_remote_copy(
        src_ref=core_out,
        dst_ref=core_in,
        send_sem=g_send.at[0],
        recv_sem=g_recv.at[0],
        device_id=sibling,
        device_id_type=MESH,
    )
    core_copy.start()
    grad[c] += dot(tok_t[...], part_s[:, half(c)])
    core_copy.wait_recv()
    ar_out[...] = (grad[c] + core_in[...].astype(F32)).astype(BF16)

    def block48(index):
        return pl.ds(pl.multiple_of(index * 48, 48), 48)

    def reduce_copy(k):
        px, py = plane_peer(k)
        return pltpu.make_async_remote_copy(
            src_ref=ar_out.at[block48(px * 4 + py)],
            dst_ref=ar_in.at[block48(mine)],
            send_sem=a_send.at[0, k],
            recv_sem=a_recv.at[0, k],
            device_id=device(px, py, z, c),
            device_id_type=MESH,
        )

    @pl.loop(1, 16)
    def _(k):
        reduce_copy(k).start()

    ar_in[block48(mine)] = ar_out[block48(mine)]
    total = acc_t[...] + dot(part, spp[...], 1, 1) + dot(disp_b[...], plane_in[3])
    for column in range(WIDTH // 128):
        gt[pl.ds(column, TOKENS, stride=WIDTH // 128), :] = total[
            0:TOKENS, 128 * column : 128 * column + 128
        ]
    gt_copy = pltpu.make_async_copy(gt, gt_hbm, o_sem.at[0, 6])
    gt_copy.start()

    @pl.loop(1, 16)
    def _(k):
        reduce_copy(k).wait_recv()

    plane_sum = ar_in[0:48].astype(F32)
    for k in range(1, 16):
        plane_sum += ar_in[48 * k : 48 * k + 48].astype(F32)
    z_out[...] = plane_sum.astype(BF16)

    def z_copy(k):
        return pltpu.make_async_remote_copy(
            src_ref=z_out,
            dst_ref=z_in.at[z],
            send_sem=z_send.at[k],
            recv_sem=z_recv.at[k],
            device_id=device(x, y, (z + k) & 7, c),
            device_id_type=MESH,
        )

    @pl.loop(1, 8)
    def _(k):
        z_copy(k).start()

    z_in[z] = z_out[...]

    @pl.loop(1, 16)
    def _(k):
        for h in range(2):
            half_copy(h, k).wait_send()
        for a in range(1, 4):
            plane_copy(a, k).wait_send()

    @pl.loop(1, 8)
    def _(k):
        for a in range(2):
            line_copy(a, k).wait_send()
            back_copy(a, k).wait_send()

    @pl.loop(0, 8)
    def _(k):
        for a in range(2):
            forward(a, k).wait_send()

    @pl.loop(0, 4)
    def _(t):
        for a in range(2):
            twin_copy(a, t).wait_send()

    core_copy.wait_send()

    @pl.loop(1, 8)
    def _(k):
        z_copy(k).wait_recv()

    line_sum = z_in[0].astype(F32)
    for k in range(1, 8):
        line_sum += z_in[k].astype(F32)
    done[c, block48(mine)] = dot(line_sum.astype(BF16), swap[0:128, 0:128]).astype(BF16)

    def gather_copy(k):
        px, py = plane_peer(k)
        return pltpu.make_async_remote_copy(
            src_ref=done.at[c, block48(mine)],
            dst_ref=done.at[c, block48(mine)],
            send_sem=a_send.at[1, k],
            recv_sem=a_recv.at[1, k],
            device_id=device(px, py, z, c),
            device_id_type=MESH,
        )

    @pl.loop(1, 16)
    def _(k):
        gather_copy(k).start()

    @pl.loop(1, 16)
    def _(k):
        reduce_copy(k).wait_send()

    @pl.loop(1, 8)
    def _(k):
        z_copy(k).wait_send()

    @pl.loop(0, HALF_HIDDEN // TILE)
    def _(j):
        out_copies(j).wait()

    @pl.loop(0, WIDTH // TILE)
    def _(j):
        in_copies(j).wait()

    gt_copy.wait()

    @pl.loop(1, 16)
    def _(k):
        gather_copy(k).wait_recv()

    last_copy = pltpu.make_async_remote_copy(
        src_ref=done.at[c],
        dst_ref=done.at[c],
        send_sem=g_send.at[1],
        recv_sem=g_recv.at[1],
        device_id=sibling,
        device_id_type=MESH,
    )
    last_copy.start()

    def result_copy(index, slot):
        return pltpu.make_async_copy(done.at[index], gsp_hbm.at[:, half(index)], g_result.at[slot])

    result_copy(c, 0).start()

    @pl.loop(1, 16)
    def _(k):
        gather_copy(k).wait_send()

    last_copy.wait()
    result_copy(c ^ 1, 1).start()
    result_copy(c, 0).wait()
    result_copy(c ^ 1, 1).wait()


def finish(gt_in, gwi_in, gwo_in, gsp_in, gt_out, gwi_out, gwo_out, gsp_out, narrow, wide, sem):
    fetch = pltpu.make_async_copy(gsp_in, narrow, sem.at[0])
    fetch.start()
    copies = [
        pltpu.make_async_copy(gwi_in, gwi_out, sem.at[1]),
        pltpu.make_async_copy(gwo_in, gwo_out, sem.at[2]),
        pltpu.make_async_copy(gt_in, gt_out, sem.at[3]),
    ]
    for copy in copies:
        copy.start()
    fetch.wait()
    wide[...] = narrow[...].astype(F32)
    last = pltpu.make_async_copy(wide, gsp_out, sem.at[4])
    last.start()
    for copy in copies:
        copy.wait()
    last.wait()


def body(tokens, grad_out, slot_param, weight_in, weight_out):
    arrays = (tokens, grad_out, slot_param, weight_in, weight_out)
    flat = (tokens.shape[1] * tokens.shape[2] // 128, 128)
    hbm = pl.BlockSpec(memory_space=pl.ANY)
    dma = pltpu.SemaphoreType.DMA
    buffers = [
        (tokens.shape, BF16),
        (tokens.shape, BF16),
        (slot_param.shape, BF16),
        ((SLOTS, SLOTS), BF16),
        ((SLOTS, SLOTS), BF16),
        ((SLOTS, SLOTS), BF16),
        ((PAD, SLOTS), BF16),
        (flat, F32),
        ((PAD, WIDTH), BF16),
        ((PAD, WIDTH), BF16),
        ((WIDTH, PAD), BF16),
        ((WIDTH, SLOTS), BF16),
        ((PAD, SLOTS), F32),
        ((PAD, SLOTS), F32),
        ((PAD, SLOTS), BF16),
        ((WIDTH, HALF_HIDDEN), BF16),
        ((HALF_HIDDEN, WIDTH), BF16),
        ((4, SLOTS, WIDTH), BF16),
        ((4, SLOTS, WIDTH), BF16),
        ((4, SLOTS, WIDTH), BF16),
        ((2, SLOTS, WIDTH), BF16),
        ((2, ROWS, WIDTH), BF16),
        ((2, NEAR, WIDTH), BF16),
        ((2, NEAR, WIDTH), BF16),
        ((2, NEAR, WIDTH), F32),
        ((ROWS, HALF_HIDDEN), BF16),
        ((ROWS, HALF_HIDDEN), F32),
        ((ROWS, HALF_HIDDEN), BF16),
        ((WIDTH, HALF_HIDDEN), BF16),
        ((HALF_HIDDEN, WIDTH), BF16),
        ((PAD, WIDTH), F32),
        ((2, WIDTH, 128), F32),
        ((WIDTH, 128), BF16),
        ((WIDTH, 128), BF16),
        ((WIDTH, 128), BF16),
        ((WIDTH, 128), BF16),
        ((48, 128), BF16),
        ((8, 48, 128), BF16),
        ((2, WIDTH, 128), BF16),
    ]
    grad_tokens, grad_in, grad_out, grad_slots = pl.pallas_call(
        kernel,
        out_shape=(
            jax.ShapeDtypeStruct(flat, F32),
            jax.ShapeDtypeStruct(weight_in.shape, BF16),
            jax.ShapeDtypeStruct(weight_out.shape, BF16),
            jax.ShapeDtypeStruct(slot_param.shape, BF16),
        ),
        in_specs=[pl.BlockSpec(memory_space=pltpu.HBM)] * 5,
        out_specs=(hbm,) * 4,
        scratch_shapes=[pltpu.VMEM(shape, kind) for shape, kind in buffers]
        + [
            dma((5,)),
            dma((2, 8)),
            dma((5, 16)),
            dma((5, 16)),
            dma((4, 8)),
            dma((4, 8)),
            dma((2, 8)),
            dma((2, 8)),
            dma((2, 4)),
            dma((2, 4)),
            dma((2, 16)),
            dma((2, 16)),
            dma((2,)),
            dma((2,)),
            dma((8,)),
            dma((8,)),
            dma((2,)),
        ],
        compiler_params=pltpu.CompilerParams(
            collective_id=0, has_side_effects=True, vmem_limit_bytes=46 * 1024 * 1024
        ),
    )(*(pltpu.with_memory_space_constraint(array, pltpu.HBM) for array in arrays))
    grad_tokens, grad_in, grad_out, grad_slots = pl.pallas_call(
        finish,
        out_shape=(
            jax.ShapeDtypeStruct(flat, F32),
            jax.ShapeDtypeStruct(weight_in.shape, BF16),
            jax.ShapeDtypeStruct(weight_out.shape, BF16),
            jax.ShapeDtypeStruct(slot_param.shape, F32),
        ),
        in_specs=[hbm] * 4,
        out_specs=(hbm,) * 4,
        scratch_shapes=[
            pltpu.VMEM(slot_param.shape, BF16),
            pltpu.VMEM(slot_param.shape, F32),
            dma((5,)),
        ],
        compiler_params=pltpu.CompilerParams(vmem_limit_bytes=8 * 1024 * 1024),
    )(grad_tokens, grad_in, grad_out, grad_slots)
    return grad_tokens.reshape(tokens.shape), grad_in, grad_out, grad_slots


def solution(mesh):
    return jax.shard_map(
        body,
        mesh=mesh,
        in_specs=(
            P(("expert", "hid"), None, None),
            P(("expert", "hid"), None, None),
            P(),
            P("expert", None, "hid"),
            P("expert", "hid", None),
        ),
        out_specs=(
            P(("expert", "hid"), None, None),
            P("expert", None, "hid"),
            P("expert", "hid", None),
            P(),
        ),
        check_vma=False,
    )
```

```python
import math

import jax
import jax.numpy as jnp
from jax import lax
from jax.experimental import pallas as pl
from jax.experimental.pallas import tpu as pltpu
from jax.sharding import PartitionSpec as P

F32 = jnp.float32
BF16 = jnp.bfloat16
MESH = pl.DeviceIdType.MESH

TOKENS = 196
PAD = 208
WIDTH = 768
HALF_HIDDEN = 1536
SLOTS = 256
ROWS = 512
NEAR = 256
BLOCK = 32
HALF = 384
TILE = 256
ROOT = math.sqrt(2.0 / math.pi)


def dot(left, right, left_dim=1, right_dim=0):
    return lax.dot_general(
        left, right, (((left_dim,), (right_dim,)), ((), ())), preferred_element_type=F32
    )


def one_hot(rows, columns, source):
    row = lax.broadcasted_iota(jnp.int32, (rows, columns), 0)
    column = lax.broadcasted_iota(jnp.int32, (rows, columns), 1)
    return jnp.where(source(row) == column, 1.0, 0.0).astype(BF16)


def swap_slots(index):
    return (index & 0xC3) | ((index & 0x30) >> 2) | ((index & 0x0C) << 2)


def to_line(index):
    return (((index >> 1) & 15) << 4) | ((index >> 5) << 1) | (index & 1)


def to_plane(index):
    return (((index >> 1) & 7) << 5) | ((index >> 4) << 1) | (index & 1)


def kernel(
    tok_hbm,
    go_hbm,
    sp_hbm,
    win_hbm,
    wout_hbm,
    gt_hbm,
    gwi_hbm,
    gwo_hbm,
    gsp_hbm,
    tok_ref,
    go_ref,
    sp_ref,
    line,
    plane,
    swap,
    part_s,
    gt,
    tok,
    go,
    tok_t,
    spp,
    disp,
    comb,
    disp_b,
    win,
    wout,
    plane_out,
    plane_in,
    line_out,
    line_in,
    rows,
    twin_out,
    twin_in,
    own,
    act,
    slope,
    gpre,
    gwi,
    gwo,
    acc_t,
    grad,
    core_out,
    core_in,
    ar_out,
    ar_in,
    z_out,
    z_in,
    done,
    w_sem,
    o_sem,
    p_send,
    p_recv,
    l_send,
    l_recv,
    f_send,
    f_recv,
    c_send,
    c_recv,
    a_send,
    a_recv,
    g_send,
    g_recv,
    z_send,
    z_recv,
    g_result,
):
    expert = lax.axis_index("expert")
    zl = lax.axis_index("hid")
    x = expert >> 5
    zh = (expert >> 3) & 3
    y = (expert >> 1) & 3
    c = expert & 1
    z = zh * 2 + zl
    mine = x * 4 + y
    side = 2 * zl - 1

    def device(px, py, pz, pc):
        return {
            "expert": (((px * 4 + (pz >> 1)) * 4 + py) * 2) + pc,
            "hid": pz & 1,
        }

    twin = device(x, y, z ^ 1, c)
    sibling = device(x, y, z, c ^ 1)

    def plane_peer(k):
        return (x + (k >> 2)) & 3, (y + (k & 3)) & 3

    i_copies = [
        pltpu.make_async_copy(sp_hbm, sp_ref, w_sem.at[2]),
        pltpu.make_async_copy(tok_hbm, tok_ref, w_sem.at[3]),
        pltpu.make_async_copy(go_hbm, go_ref, w_sem.at[4]),
    ]
    w_copies = [
        pltpu.make_async_copy(win_hbm.at[0], win, w_sem.at[0]),
        pltpu.make_async_copy(wout_hbm.at[0], wout, w_sem.at[1]),
    ]
    for copy in i_copies + w_copies:
        copy.start()

    barrier = pltpu.get_barrier_semaphore()

    @pl.loop(1, 16)
    def _(k):
        px, py = plane_peer(k)
        pl.semaphore_signal(barrier, inc=1, device_id=device(px, py, z, c), device_id_type=MESH)
        pl.semaphore_signal(
            barrier,
            inc=1,
            device_id=device(x, y, (z + (k >> 1)) & 7, c ^ (k & 1)),
            device_id_type=MESH,
        )

    def block16(index):
        return pl.ds(pl.multiple_of(index * 16, 16), 16)

    def block32(index):
        return pl.ds(pl.multiple_of(index * BLOCK, BLOCK), BLOCK)

    def plane_copy(a, k):
        px, py = plane_peer(k)
        return pltpu.make_async_remote_copy(
            src_ref=plane_out.at[a, block16(px * 4 + py)],
            dst_ref=plane_in.at[a, block16(mine)],
            send_sem=p_send.at[a, k],
            recv_sem=p_recv.at[a, k],
            device_id=device(px, py, z, c),
            device_id_type=MESH,
        )

    def half_copy(h, k):
        px, py = plane_peer(k)
        columns = pl.ds(h * HALF, HALF)
        return pltpu.make_async_remote_copy(
            src_ref=plane_out.at[0, block16(px * 4 + py), columns],
            dst_ref=plane_in.at[0, block16(mine), columns],
            send_sem=p_send.at[4 * h, k],
            recv_sem=p_recv.at[4 * h, k],
            device_id=device(px, py, z, c),
            device_id_type=MESH,
        )

    def half_start(h):
        @pl.loop(1, 16, unroll=5)
        def _(k):
            half_copy(h, k).start()

        columns = pl.ds(h * HALF, HALF)
        plane_in[0, block16(mine), columns] = plane_out[0, block16(mine), columns]

    def half_finish(h):
        @pl.loop(1, 16)
        def _(k):
            half_copy(h, k).wait_recv()

    def plane_start(a):
        @pl.loop(1, 16, unroll=5)
        def _(k):
            plane_copy(a, k).start()

        plane_in[a, block16(mine)] = plane_out[a, block16(mine)]

    def plane_finish(a):
        @pl.loop(1, 16)
        def _(k):
            plane_copy(a, k).wait_recv()

    def line_copy(a, j, columns=pl.ds(0, WIDTH)):
        q = (zh + (j >> 1)) & 3
        pc = c ^ (j & 1)
        k = (z - 2 * q + 11) & 7
        low = k >> 2
        far = jnp.where(low == 1, k - 4, 3 - k)
        return pltpu.make_async_remote_copy(
            src_ref=line_out.at[a, block32(q * 2 + pc), columns],
            dst_ref=rows.at[a, block32(k * 2 + c), columns],
            send_sem=l_send.at[a, j],
            recv_sem=l_recv.at[a, far * 2 + (j & 1)],
            device_id=device(x, y, 2 * q + low, pc),
            device_id_type=MESH,
        )

    def near_row(t, pc):
        return (3 + zl + side * t) * 2 + pc

    def own_copy(a, j, columns):
        pc = c ^ j
        return pltpu.make_async_remote_copy(
            src_ref=line_out.at[a, block32(zh * 2 + pc), columns],
            dst_ref=rows.at[a, block32((3 + zl) * 2 + c), columns],
            send_sem=f_send.at[a, j],
            recv_sem=f_recv.at[a, j],
            device_id=device(x, y, z ^ 1, pc),
            device_id_type=MESH,
        )

    def line_start(a, columns=pl.ds(0, WIDTH)):
        for dq in (1, 3):
            for dc in range(2):
                line_copy(a, 2 * dq + dc, columns).start()
        line_copy(a, 1, columns).start()
        for dc in range(2):
            own_copy(a, dc, columns).start()
        for dc in range(2):
            line_copy(a, 4 + dc, columns).start()
        rows[a, block32((3 + zl) * 2 + c), columns] = line_out[a, block32(zh * 2 + c), columns]

    def arrive(a, j):
        place = block32(near_row(j >> 1, c ^ (j & 1)))
        return pltpu.make_async_remote_copy(
            src_ref=rows.at[a, place],
            dst_ref=rows.at[a, place],
            send_sem=f_send.at[a, j],
            recv_sem=l_recv.at[a, j],
            device_id=twin,
            device_id_type=MESH,
        )

    def forward(a, j):
        place = block32(near_row(j >> 1, c ^ (j & 1)))
        return pltpu.make_async_remote_copy(
            src_ref=rows.at[a, place],
            dst_ref=rows.at[a, place],
            send_sem=f_send.at[a, j],
            recv_sem=f_recv.at[a, j],
            device_id=twin,
            device_id_type=MESH,
        )

    def pass_on(a, t):
        for dc in range(2):
            j = 2 * t + dc
            arrive(a, j).wait_recv()
            forward(a, j).start()

    def own_finish(a):
        arrive(a, 1).wait_recv()

    def far_finish(a):
        @pl.loop(0, 8)
        def _(j):
            forward(a, j).wait_recv()

    def near_chunk(low, t):
        return 3 - 3 * low + (2 * low - 1) * t

    def twin_copy(a, t):
        place = pl.ds(pl.multiple_of(near_chunk(1 - zl, t) * 64, 64), 64)
        return pltpu.make_async_remote_copy(
            src_ref=twin_out.at[a, place],
            dst_ref=twin_in.at[a, place],
            send_sem=c_send.at[a, t],
            recv_sem=c_recv.at[a, t],
            device_id=twin,
            device_id_type=MESH,
        )

    def back_copy(a, j):
        t = j >> 1
        pc = c ^ (j & 1)
        pz = (z + side * t + 8) & 7
        shift = (zh - (pz >> 1) + 4) & 3
        return pltpu.make_async_remote_copy(
            src_ref=line_out.at[2 + a, block32(near_row(t, pc) - 8 * zl)],
            dst_ref=line_in.at[a, block32(zh * 2 + c)],
            send_sem=l_send.at[2 + a, j],
            recv_sem=l_recv.at[2 + a, shift * 2 + (j & 1)],
            device_id=device(x, y, pz, pc),
            device_id_type=MESH,
        )

    near_rows = pl.ds(pl.multiple_of(zl * NEAR, NEAR), NEAR)
    far_rows = pl.ds(pl.multiple_of((1 - zl) * NEAR, NEAR), NEAR)

    def back_finish(a):
        @pl.loop(1, 8)
        def _(j):
            pltpu.make_async_remote_copy(
                src_ref=line_in.at[a, block32(0)],
                dst_ref=line_in.at[a, block32(0)],
                send_sem=l_send.at[2 + a, j],
                recv_sem=l_recv.at[2 + a, j],
                device_id=twin,
                device_id_type=MESH,
            ).wait_recv()

    swap[...] = one_hot(SLOTS, SLOTS, swap_slots)
    tok[TOKENS - 4 :, :] = jnp.zeros((PAD - TOKENS + 4, WIDTH), BF16)
    go[TOKENS - 4 :, :] = jnp.zeros((PAD - TOKENS + 4, WIDTH), BF16)
    i_copies[0].wait()
    spp[...] = dot(sp_ref[...], swap[...]).astype(BF16)
    i_copies[1].wait()
    tok[0:TOKENS, :] = tok_ref[0]
    logits = dot(tok[...], spp[...])
    valid = lax.broadcasted_iota(jnp.int32, (PAD, SLOTS), 0) < TOKENS
    masked = jnp.where(valid, logits, -1e30)
    raised = jnp.exp(masked - jnp.max(masked, axis=0, keepdims=True))
    dispatch = raised / jnp.sum(raised, axis=0, keepdims=True)
    disp[...] = dispatch
    disp_b[...] = dispatch.astype(BF16)
    plane_out[0, :, 0:HALF] = dot(disp_b[...], tok[:, 0:HALF], 0, 0).astype(BF16)
    pl.semaphore_wait(barrier, 30)
    half_start(0)
    plane_out[0, :, HALF:WIDTH] = dot(disp_b[...], tok[:, HALF:WIDTH], 0, 0).astype(BF16)
    half_start(1)
    i_copies[2].wait()
    go[0:TOKENS, :] = go_ref[0]
    raised = jnp.exp(logits - jnp.max(logits, axis=1, keepdims=True))
    combine = raised / jnp.sum(raised, axis=1, keepdims=True)
    comb[...] = combine
    plane_out[1] = dot(combine.astype(BF16), go[...], 0, 0).astype(BF16)
    plane_start(1)
    line[...] = one_hot(SLOTS, SLOTS, to_line)
    for h in range(2):
        half_finish(h)
        columns = pl.ds(h * HALF, HALF)
        line_out[0, :, columns] = dot(line[...], plane_in[0, :, columns]).astype(BF16)
        line_start(0, columns)
    plane[...] = one_hot(SLOTS, SLOTS, to_plane)
    tok_t[...] = tok[...].T
    pass_on(0, 1)
    plane_finish(1)
    line_out[1] = dot(line[...], plane_in[1]).astype(BF16)
    line_start(1)
    pass_on(0, 2)
    pass_on(0, 3)
    own_finish(0)
    for copy in w_copies:
        copy.wait()

    def activate(place):
        @pl.loop(0, HALF_HIDDEN // TILE)
        def _(j):
            tile = pl.ds(pl.multiple_of(j * TILE, TILE), TILE)
            pre = dot(rows[0, place], win[:, tile])
            square = pre * pre
            tanh = jnp.tanh(ROOT * pre * (1.0 + 0.044715 * square))
            half = 0.5 * (1.0 + tanh)
            act[place, tile] = (pre * half).astype(BF16)
            slope[place, tile] = half + (0.5 * ROOT) * pre * (1.0 - tanh * tanh) * (
                1.0 + (3 * 0.044715) * square
            )

    def twin_rows(wide, weight, weight_dim, place, target, cast):
        @pl.loop(0, WIDTH // TILE)
        def _(j):
            tile = pl.ds(pl.multiple_of(j * TILE, TILE), TILE)
            if weight_dim == 0:
                value = dot(wide[place], weight[:, tile])
            else:
                value = dot(wide[place], weight[tile, :], 1, 1)
            target[:, tile] = value.astype(cast)

    def sum_back(a, t):
        twin_copy(a, t).wait_recv()
        place = pl.ds(pl.multiple_of(near_chunk(zl, t) * 64, 64), 64)
        line_out[2 + a, place] = (own[a, place] + twin_in[a, place].astype(F32)).astype(BF16)
        back_copy(a, 2 * t + 1).start()
        if t > 0:
            back_copy(a, 2 * t).start()
        else:
            line_in[a, block32(zh * 2 + c)] = line_out[2 + a, block32(near_row(0, c) - 8 * zl)]

    pass_on(1, 1)
    activate(near_rows)
    pass_on(1, 2)
    pass_on(1, 3)
    own_finish(1)
    far_finish(0)
    activate(far_rows)
    twin_rows(act, wout, 0, far_rows, twin_out.at[0], BF16)
    for t in (3, 2, 1, 0):
        twin_copy(0, t).start()
    twin_rows(act, wout, 0, near_rows, own.at[0], F32)

    def pull(place):
        @pl.loop(0, HALF_HIDDEN // TILE)
        def _(j):
            tile = pl.ds(pl.multiple_of(j * TILE, TILE), TILE)
            gpre[place, tile] = (dot(rows[1, place], wout[tile, :], 1, 1) * slope[place, tile]).astype(
                BF16
            )

    pull(near_rows)
    twin_rows(gpre, win, 1, near_rows, own.at[1], F32)
    far_finish(1)
    pull(far_rows)
    twin_rows(gpre, win, 1, far_rows, twin_out.at[1], BF16)
    for t in (3, 2, 1, 0):
        sum_back(0, t)
        twin_copy(1, t).start()

    def out_copies(j):
        tile = pl.ds(pl.multiple_of(j * TILE, TILE), TILE)
        return pltpu.make_async_copy(gwo.at[tile], gwo_hbm.at[0, tile], o_sem.at[0, j])

    def in_copies(j):
        tile = pl.ds(pl.multiple_of(j * TILE, TILE), TILE)
        return pltpu.make_async_copy(gwi.at[tile], gwi_hbm.at[0, tile], o_sem.at[1, j])

    sum_back(1, 3)
    sum_back(1, 2)
    back_finish(0)
    plane_out[2] = dot(plane[...], line_in[0]).astype(BF16)
    plane_start(2)
    sum_back(1, 1)
    sum_back(1, 0)
    plane_finish(2)
    gc = dot(go[...], plane_in[2], 1, 1)
    weight = comb[...]
    part = (weight * (gc - jnp.sum(gc * weight, axis=1, keepdims=True))).astype(BF16)
    acc_t[...] = dot(part, spp[...], 1, 1)
    grad_half = dot(tok_t[...], part)
    grad[0] = grad_half[:, 0:128]
    grad[1] = grad_half[:, 128:256]

    back_finish(1)
    plane_out[3] = dot(plane[...], line_in[1]).astype(BF16)
    plane_start(3)

    @pl.loop(0, HALF_HIDDEN // TILE)
    def _(j):
        tile = pl.ds(pl.multiple_of(j * TILE, TILE), TILE)
        gwo[tile, :] = dot(act[:, tile], rows[1], 0, 0).astype(BF16)
        out_copies(j).start()

    @pl.loop(0, WIDTH // TILE)
    def _(j):
        tile = pl.ds(pl.multiple_of(j * TILE, TILE), TILE)
        gwi[tile, :] = dot(rows[0, :, tile], gpre[...], 0, 0).astype(BF16)
        in_copies(j).start()

    plane_finish(3)
    gd = dot(tok[...], plane_in[3], 1, 1)
    weight = disp[...]
    part = (weight * (gd - jnp.sum(gd * weight, axis=0, keepdims=True))).astype(BF16)
    part_s[...] = part

    def half(index):
        return pl.ds(pl.multiple_of(index * 128, 128), 128)

    other = dot(tok_t[...], part_s[:, half(c ^ 1)])
    core_out[...] = (grad[c ^ 1] + other).astype(BF16)
    core_copy = pltpu.make_async_remote_copy(
        src_ref=core_out,
        dst_ref=core_in,
        send_sem=g_send.at[0],
        recv_sem=g_recv.at[0],
        device_id=sibling,
        device_id_type=MESH,
    )
    core_copy.start()
    grad[c] += dot(tok_t[...], part_s[:, half(c)])
    core_copy.wait_recv()
    ar_out[...] = (grad[c] + core_in[...].astype(F32)).astype(BF16)

    def block48(index):
        return pl.ds(pl.multiple_of(index * 48, 48), 48)

    def reduce_copy(k):
        px, py = plane_peer(k)
        return pltpu.make_async_remote_copy(
            src_ref=ar_out.at[block48(px * 4 + py)],
            dst_ref=ar_in.at[block48(mine)],
            send_sem=a_send.at[0, k],
            recv_sem=a_recv.at[0, k],
            device_id=device(px, py, z, c),
            device_id_type=MESH,
        )

    @pl.loop(1, 16, unroll=5)
    def _(k):
        reduce_copy(k).start()

    ar_in[block48(mine)] = ar_out[block48(mine)]
    total = acc_t[...] + dot(part, spp[...], 1, 1) + dot(disp_b[...], plane_in[3])
    for column in range(WIDTH // 128):
        gt[pl.ds(column, TOKENS, stride=WIDTH // 128), :] = total[
            0:TOKENS, 128 * column : 128 * column + 128
        ]
    gt_copy = pltpu.make_async_copy(gt, gt_hbm, o_sem.at[0, 6])
    gt_copy.start()

    @pl.loop(1, 16, unroll=5)
    def _(k):
        reduce_copy(k).wait_recv()

    plane_sum = ar_in[0:48].astype(F32)
    for k in range(1, 16):
        plane_sum += ar_in[48 * k : 48 * k + 48].astype(F32)
    z_out[...] = plane_sum.astype(BF16)

    def z_copy(k):
        return pltpu.make_async_remote_copy(
            src_ref=z_out,
            dst_ref=z_in.at[z],
            send_sem=z_send.at[k],
            recv_sem=z_recv.at[k],
            device_id=device(x, y, (z + k) & 7, c),
            device_id_type=MESH,
        )

    @pl.loop(1, 8)
    def _(k):
        z_copy(k).start()

    z_in[z] = z_out[...]

    @pl.loop(1, 16)
    def _(k):
        for h in range(2):
            half_copy(h, k).wait_send()
        for a in range(1, 4):
            plane_copy(a, k).wait_send()

    @pl.loop(1, 8)
    def _(k):
        for a in range(2):
            line_copy(a, k).wait_send()
            back_copy(a, k).wait_send()

    @pl.loop(0, 8)
    def _(k):
        for a in range(2):
            forward(a, k).wait_send()

    @pl.loop(0, 4)
    def _(t):
        for a in range(2):
            twin_copy(a, t).wait_send()

    core_copy.wait_send()

    @pl.loop(1, 8)
    def _(k):
        z_copy(k).wait_recv()

    line_sum = z_in[0].astype(F32)
    for k in range(1, 8):
        line_sum += z_in[k].astype(F32)
    done[c, block48(mine)] = dot(line_sum.astype(BF16), swap[0:128, 0:128]).astype(BF16)

    def gather_copy(k):
        px, py = plane_peer(k)
        return pltpu.make_async_remote_copy(
            src_ref=done.at[c, block48(mine)],
            dst_ref=done.at[c, block48(mine)],
            send_sem=a_send.at[1, k],
            recv_sem=a_recv.at[1, k],
            device_id=device(px, py, z, c),
            device_id_type=MESH,
        )

    @pl.loop(1, 16, unroll=5)
    def _(k):
        gather_copy(k).start()

    @pl.loop(1, 16)
    def _(k):
        reduce_copy(k).wait_send()

    @pl.loop(1, 8)
    def _(k):
        z_copy(k).wait_send()

    @pl.loop(0, HALF_HIDDEN // TILE)
    def _(j):
        out_copies(j).wait()

    @pl.loop(0, WIDTH // TILE)
    def _(j):
        in_copies(j).wait()

    gt_copy.wait()

    @pl.loop(1, 16, unroll=5)
    def _(k):
        gather_copy(k).wait_recv()

    last_copy = pltpu.make_async_remote_copy(
        src_ref=done.at[c],
        dst_ref=done.at[c],
        send_sem=g_send.at[1],
        recv_sem=g_recv.at[1],
        device_id=sibling,
        device_id_type=MESH,
    )
    last_copy.start()

    def result_copy(index, slot):
        return pltpu.make_async_copy(done.at[index], gsp_hbm.at[:, half(index)], g_result.at[slot])

    result_copy(c, 0).start()

    @pl.loop(1, 16)
    def _(k):
        gather_copy(k).wait_send()

    last_copy.wait()
    result_copy(c ^ 1, 1).start()
    result_copy(c, 0).wait()
    result_copy(c ^ 1, 1).wait()


def finish(gt_in, gwi_in, gwo_in, gsp_in, gt_out, gwi_out, gwo_out, gsp_out, narrow, wide, sem):
    fetch = pltpu.make_async_copy(gsp_in, narrow, sem.at[0])
    fetch.start()
    copies = [
        pltpu.make_async_copy(gwi_in, gwi_out, sem.at[1]),
        pltpu.make_async_copy(gwo_in, gwo_out, sem.at[2]),
        pltpu.make_async_copy(gt_in, gt_out, sem.at[3]),
    ]
    for copy in copies:
        copy.start()
    fetch.wait()
    wide[...] = narrow[...].astype(F32)
    last = pltpu.make_async_copy(wide, gsp_out, sem.at[4])
    last.start()
    for copy in copies:
        copy.wait()
    last.wait()


def body(tokens, grad_out, slot_param, weight_in, weight_out):
    arrays = (tokens, grad_out, slot_param, weight_in, weight_out)
    flat = (tokens.shape[1] * tokens.shape[2] // 128, 128)
    hbm = pl.BlockSpec(memory_space=pl.ANY)
    dma = pltpu.SemaphoreType.DMA
    buffers = [
        (tokens.shape, BF16),
        (tokens.shape, BF16),
        (slot_param.shape, BF16),
        ((SLOTS, SLOTS), BF16),
        ((SLOTS, SLOTS), BF16),
        ((SLOTS, SLOTS), BF16),
        ((PAD, SLOTS), BF16),
        (flat, F32),
        ((PAD, WIDTH), BF16),
        ((PAD, WIDTH), BF16),
        ((WIDTH, PAD), BF16),
        ((WIDTH, SLOTS), BF16),
        ((PAD, SLOTS), F32),
        ((PAD, SLOTS), F32),
        ((PAD, SLOTS), BF16),
        ((WIDTH, HALF_HIDDEN), BF16),
        ((HALF_HIDDEN, WIDTH), BF16),
        ((4, SLOTS, WIDTH), BF16),
        ((4, SLOTS, WIDTH), BF16),
        ((4, SLOTS, WIDTH), BF16),
        ((2, SLOTS, WIDTH), BF16),
        ((2, ROWS, WIDTH), BF16),
        ((2, NEAR, WIDTH), BF16),
        ((2, NEAR, WIDTH), BF16),
        ((2, NEAR, WIDTH), F32),
        ((ROWS, HALF_HIDDEN), BF16),
        ((ROWS, HALF_HIDDEN), F32),
        ((ROWS, HALF_HIDDEN), BF16),
        ((WIDTH, HALF_HIDDEN), BF16),
        ((HALF_HIDDEN, WIDTH), BF16),
        ((PAD, WIDTH), F32),
        ((2, WIDTH, 128), F32),
        ((WIDTH, 128), BF16),
        ((WIDTH, 128), BF16),
        ((WIDTH, 128), BF16),
        ((WIDTH, 128), BF16),
        ((48, 128), BF16),
        ((8, 48, 128), BF16),
        ((2, WIDTH, 128), BF16),
    ]
    grad_tokens, grad_in, grad_out, grad_slots = pl.pallas_call(
        kernel,
        out_shape=(
            jax.ShapeDtypeStruct(flat, F32),
            jax.ShapeDtypeStruct(weight_in.shape, BF16),
            jax.ShapeDtypeStruct(weight_out.shape, BF16),
            jax.ShapeDtypeStruct(slot_param.shape, BF16),
        ),
        in_specs=[pl.BlockSpec(memory_space=pltpu.HBM)] * 5,
        out_specs=(hbm,) * 4,
        scratch_shapes=[pltpu.VMEM(shape, kind) for shape, kind in buffers]
        + [
            dma((5,)),
            dma((2, 8)),
            dma((5, 16)),
            dma((5, 16)),
            dma((4, 8)),
            dma((4, 8)),
            dma((2, 8)),
            dma((2, 8)),
            dma((2, 4)),
            dma((2, 4)),
            dma((2, 16)),
            dma((2, 16)),
            dma((2,)),
            dma((2,)),
            dma((8,)),
            dma((8,)),
            dma((2,)),
        ],
        compiler_params=pltpu.CompilerParams(
            collective_id=0, has_side_effects=True, vmem_limit_bytes=46 * 1024 * 1024
        ),
    )(*(pltpu.with_memory_space_constraint(array, pltpu.HBM) for array in arrays))
    grad_tokens, grad_in, grad_out, grad_slots = pl.pallas_call(
        finish,
        out_shape=(
            jax.ShapeDtypeStruct(flat, F32),
            jax.ShapeDtypeStruct(weight_in.shape, BF16),
            jax.ShapeDtypeStruct(weight_out.shape, BF16),
            jax.ShapeDtypeStruct(slot_param.shape, F32),
        ),
        in_specs=[hbm] * 4,
        out_specs=(hbm,) * 4,
        scratch_shapes=[
            pltpu.VMEM(slot_param.shape, BF16),
            pltpu.VMEM(slot_param.shape, F32),
            dma((5,)),
        ],
        compiler_params=pltpu.CompilerParams(vmem_limit_bytes=8 * 1024 * 1024),
    )(grad_tokens, grad_in, grad_out, grad_slots)
    return grad_tokens.reshape(tokens.shape), grad_in, grad_out, grad_slots


def solution(mesh):
    return jax.shard_map(
        body,
        mesh=mesh,
        in_specs=(
            P(("expert", "hid"), None, None),
            P(("expert", "hid"), None, None),
            P(),
            P("expert", None, "hid"),
            P("expert", "hid", None),
        ),
        out_specs=(
            P(("expert", "hid"), None, None),
            P("expert", None, "hid"),
            P("expert", "hid", None),
            P(),
        ),
        check_vma=False,
    )
```
